32 devices in a mesh: dp: 16 (over z, y, x), chan: 2 (over core).
Axes of the slice: x: 2, y: 2, z: 4, core: 2. Of those that a mesh axis runs over, the one named last changes fastest.
Arguments:
- frames: bfloat16 [256, 67600], P('chan', 'dp'), may hold values from -6 to 6
- clip_counts: int32 [16], P('dp'), may hold values from 1 to 25, as said below
- conv3_weight: bfloat16 [512, 2304], P('chan'), may hold values from -0.125 to 0.125
- conv3_bias: bfloat16 [512], P('chan'), may hold values from -3 to 3
- conv4_weight: bfloat16 [512, 4608], P('chan'), may hold values from -0.09375 to 0.09375
- conv4_bias: bfloat16 [512], P('chan'), may hold values from -3 to 3
- cotangent: bfloat16 [512, 67600], P('chan', 'dp'), may hold values from -6 to 6
Outputs:
- conv4_out: bfloat16 [512, 67600], P('chan', 'dp')
- frames_grad: float32 [256, 67600], P('chan', 'dp')
- conv3_weight_grad: float32 [512, 2304], P('chan')
- conv3_bias_grad: float32 [512], P('chan')
- conv4_weight_grad: float32 [512, 4608], P('chan')
- conv4_bias_grad: float32 [512], P('chan')
The draws below stay inside these ranges and needn't reach their ends.
Inputs may be any that keep to these rules, and one draw needn't show every extreme that they name: Frame slots v * 25 to v * 25 + clip_counts[v] - 1 are live; some video has 25 live frames and some has 1.
All inputs are finite; a program needn't handle non-finite values.
Results may differ from the reference program's by a relative error of at most 0.0055.
Values may be sent and summed in bfloat16 or wider, within the bound.
A program may use at most 256 MiB of HBM per device.

```python
import jax
import jax.numpy as jnp
from jax import lax

C_IN = 256
C_MID = 512
MAP = 13
CLIPS = 25
VIDEOS = 16
FRAMES = 400
N_DP = 16


def draw_clip_counts(key, part):
    key = jax.random.fold_in(key, 7)
    first, second = jax.random.split(key)
    counts = jax.random.randint(first, (VIDEOS,), 1, CLIPS + 1)
    spots = jax.random.permutation(second, VIDEOS)
    counts = counts.at[spots[0]].set(CLIPS)
    counts = counts.at[spots[1]].set(1)
    return counts.astype(jnp.int32)


def steps_of(stream_key, dims, shards, least, largest):
    level, own = 1.0, jax.random.fold_in(stream_key, 6)
    for dim, blocks in shards:
        draws = jnp.exp(jax.random.uniform(jax.random.fold_in(own, dim), (blocks,), jnp.float32, least / len(shards), largest / len(shards)))
        level = level * jnp.repeat(draws, dims[dim] // blocks).reshape([-1 if axis == dim else 1 for axis in range(len(dims))])
    return level


def gaussian(stream_key, extent, width, limit, cuts=(), kind=jnp.bfloat16):
    array = width * jax.random.normal(stream_key, extent, jnp.float32)
    if cuts:
        array = array * steps_of(stream_key, extent, cuts, -0.22, 0.18)
    return jnp.clip(array, -limit, limit).astype(kind)


def setup_inputs(seed: int = 0) -> dict:
    key_of = jax.random.split(jax.random.key(seed), 8)
    return {
        "frames": gaussian(key_of[0], (C_IN, FRAMES * MAP * MAP), 1.0, 6.0, ((0, 2), (1, 16))),
        "clip_counts": draw_clip_counts(jax.random.fold_in(key_of[7], 71), 0),
        "conv3_weight": gaussian(key_of[2], (C_MID, 9 * C_IN), (9 * C_IN) ** -0.5, 0.125, ((0, 2),)),
        "conv3_bias": gaussian(key_of[3], (C_MID,), 0.5, 3.0, ((0, 2),)),
        "conv4_weight": gaussian(key_of[4], (C_MID, 9 * C_MID), (9 * C_MID) ** -0.5, 0.09375, ((0, 2),)),
        "conv4_bias": gaussian(key_of[5], (C_MID,), 0.5, 3.0, ((0, 2),)),
        "cotangent": gaussian(key_of[6], (C_MID, FRAMES * MAP * MAP), 1.0, 6.0, ((0, 2), (1, 16))),
    }


@jax.custom_vjp
def low(v):
    return lax.optimization_barrier(v.astype(jnp.bfloat16)).astype(jnp.float32)

@jax.custom_vjp
def low_back(v):
    return v

def low_keep(v):
    return (low(v), None)

def low_pass(kept, grad):
    return (grad,)

def back_keep(v):
    return (v, None)

def back_low(kept, grad):
    return (low(grad),)
low.defvjp(low_keep, low_pass)
low_back.defvjp(back_keep, back_low)

def convolve(field, kernel):
    padded = jnp.pad(field, ((0, 0), (1, 1), (1, 1), (0, 0)))
    result = None
    for tap_row in range(3):
        for tap_col in range(3):
            window = padded[:, tap_row:tap_row + MAP, tap_col:tap_col + MAP, :]
            term = jnp.einsum('nhwc,cd->nhwd', window, kernel[tap_row, tap_col], precision=lax.Precision.HIGHEST)
            result = term if result is None else result + term
    return result

def to_maps(flat, channels):
    return flat.reshape(channels, -1, MAP, MAP).transpose(1, 2, 3, 0)

def to_flat(maps):
    return maps.transpose(3, 0, 1, 2).reshape(maps.shape[3], -1)

def to_hwio(kernel, channels):
    return kernel.reshape(-1, 3, 3, channels).transpose(1, 2, 3, 0)

def layer_pair(field, kernel3, bias3, kernel4, bias4, alive_mask):
    inputs = to_maps(field, C_IN)
    pre3 = convolve(inputs, to_hwio(kernel3, C_IN)) + bias3
    mid = low(jax.nn.silu(low_back(pre3)))
    pre4 = convolve(mid, to_hwio(kernel4, C_MID)) + bias4
    return to_flat(alive_mask * jax.nn.silu(low_back(pre4)))

def reference(frames, clip_counts, conv3_weight, conv3_bias, conv4_weight, conv4_bias, cotangent):
    blocks = N_DP
    per_block = FRAMES // blocks
    width_block = per_block * MAP * MAP
    slots = jnp.arange(CLIPS, dtype=jnp.int32)
    alive = (slots[None, :] < clip_counts[:, None]).astype(jnp.float32).reshape(blocks, per_block, 1, 1, 1)
    inputs = frames.astype(jnp.float32).reshape(C_IN, blocks, width_block).transpose(1, 0, 2)
    incoming = cotangent.astype(jnp.float32).reshape(C_MID, blocks, width_block).transpose(1, 0, 2)
    params = tuple((item.astype(jnp.float32) for item in (conv3_weight, conv3_bias, conv4_weight, conv4_bias)))
    zeros = tuple((jnp.zeros_like(item) for item in params))

    def advance(running, piece):
        block_x, block_alive, block_ct = piece

        def forward(field, kernel3, bias3, kernel4, bias4):
            return layer_pair(field, kernel3, bias3, kernel4, bias4, block_alive)
        result, pull = jax.vjp(forward, block_x, *params)
        grads = pull(block_ct)
        running = tuple((left + right for left, right in zip(running, grads[1:])))
        return (running, (result.astype(jnp.bfloat16), grads[0]))
    running, (outputs, input_grads) = lax.scan(advance, zeros, (inputs, alive, incoming))
    conv4_out = outputs.transpose(1, 0, 2).reshape(C_MID, FRAMES * MAP * MAP)
    frames_grad = input_grads.transpose(1, 0, 2).reshape(C_IN, FRAMES * MAP * MAP)
    return (conv4_out, frames_grad, running[0], running[1], running[2], running[3])
```

```python
import functools

import jax
import jax.numpy as jnp
from jax import lax
from jax.experimental import pallas as pl
from jax.experimental.pallas import tpu as pltpu
from jax.sharding import PartitionSpec as P

MAP = 13
AREA = MAP * MAP
LANES = 128
WINDOW = 256
BATCH = 8
MESH = pl.DeviceIdType.MESH
F32 = jnp.float32
BF16 = jnp.bfloat16
MIB = 2**20


def shift_cols(values, offset):
    if offset == 0:
        return values
    if offset > 0:
        return jnp.pad(values[:, offset:], ((0, 0), (0, offset)))
    return jnp.pad(values[:, :offset], ((0, 0), (-offset, 0)))


def tap_table(count):
    pixel = jnp.arange(count, dtype=jnp.int32) % AREA
    row_of = pixel // MAP
    col_of = pixel % MAP
    table = []
    for tap in range(9):
        tap_row = tap // 3
        tap_col = tap % 3
        src_row = row_of + tap_row - 1
        src_col = col_of + tap_col - 1
        valid = (src_row >= 0) & (src_row < MAP) & (src_col >= 0) & (src_col < MAP)
        table.append(((tap_row - 1) * MAP + tap_col - 1, valid[None, :]))
    return table


def conv_forward(field, kernel, table):
    result = None
    for tap in range(9):
        offset, valid = table[tap]
        term = jnp.dot(kernel[:, tap, :], field, preferred_element_type=F32)
        term = jnp.where(valid, shift_cols(term, offset), 0.0)
        result = term if result is None else result + term
    return result


def conv_backward(grad_field, kernel, table):
    result = None
    for tap in range(9):
        offset, valid = table[tap]
        masked = jnp.where(valid, grad_field, jnp.zeros((), grad_field.dtype))
        moved = shift_cols(masked, -offset)
        term = jnp.einsum("dc,dp->cp", kernel[:, tap, :], moved, preferred_element_type=F32)
        result = term if result is None else result + term
    return result


def kernel_grad(field, grad_field, table):
    taps_out = []
    for tap in range(9):
        offset, valid = table[tap]
        masked = jnp.where(valid, grad_field, jnp.zeros((), grad_field.dtype))
        moved = shift_cols(masked, -offset)
        taps_out.append(jnp.einsum("dp,cp->dc", moved, field, preferred_element_type=F32))
    return jnp.concatenate(taps_out, axis=1)


def silu_slope(value, sigma):
    return sigma * (1.0 + value * (1.0 - sigma))


def unpack(flat, shapes):
    pieces = []
    offset = 0
    for shape in shapes:
        length = 1
        for extent in shape:
            length = length * extent
        pieces.append(flat[offset : offset + length].reshape(shape))
        offset = offset + length
    return pieces


def general_device(frames, clip_counts, conv3_weight, conv3_bias, conv4_weight, conv4_bias, cotangent):
    columns = frames.shape[1]
    frame_count = columns // AREA
    videos_here = clip_counts.shape[0]
    per_video = frame_count // videos_here
    out_width = conv3_weight.shape[0]
    frame_ids = jnp.arange(frame_count, dtype=jnp.int32)
    owner = (frame_ids // per_video)[:, None] == jnp.arange(videos_here, dtype=jnp.int32)[None, :]
    count_of = jnp.sum(jnp.where(owner, clip_counts[None, :], 0), axis=1)
    frame_alive = (frame_ids % per_video < count_of).astype(F32)
    alive = jnp.broadcast_to(frame_alive[:, None], (frame_count, AREA)).reshape(1, columns)
    table = tap_table(columns)
    kernel3 = conv3_weight.reshape(out_width, 9, -1)
    kernel4 = conv4_weight.reshape(out_width, 9, -1)
    full_input = lax.all_gather(frames, "chan", axis=0, tiled=True)
    pre3 = conv_forward(full_input, kernel3, table) + conv3_bias.astype(F32)[:, None]
    sigma3 = jax.nn.sigmoid(pre3)
    mid = (pre3 * sigma3).astype(BF16)
    full_mid = lax.all_gather(mid, "chan", axis=0, tiled=True)
    pre4 = conv_forward(full_mid, kernel4, table) + conv4_bias.astype(F32)[:, None]
    sigma4 = jax.nn.sigmoid(pre4)
    conv4_out = (alive * pre4 * sigma4).astype(BF16)
    grad4 = (cotangent.astype(F32) * alive * silu_slope(pre4, sigma4)).astype(BF16)
    kernel4_local = kernel_grad(full_mid, grad4, table)
    bias4_local = jnp.sum(grad4.astype(F32), axis=1)
    shapes4 = (kernel4_local.shape, bias4_local.shape)
    partial_terms = conv_backward(grad4, kernel4, table)
    grad_mid = lax.psum_scatter(partial_terms, "chan", scatter_dimension=0, tiled=True)
    grad3 = (grad_mid * silu_slope(pre3, sigma3)).astype(BF16)
    kernel3_local = kernel_grad(full_input, grad3, table)
    bias3_local = jnp.sum(grad3.astype(F32), axis=1)
    shapes3 = (kernel3_local.shape, bias3_local.shape)
    input_terms = conv_backward(grad3, kernel3, table)
    frames_grad = lax.psum_scatter(input_terms, "chan", scatter_dimension=0, tiled=True)
    packed = jnp.concatenate(
        [item.reshape(-1) for item in (kernel3_local, bias3_local, kernel4_local, bias4_local)]
    )
    whole = lax.psum(packed, "dp")
    conv3_weight_grad, conv3_bias_grad, conv4_weight_grad, conv4_bias_grad = unpack(
        whole, shapes3 + shapes4
    )
    return (
        conv4_out,
        frames_grad,
        conv3_weight_grad,
        conv3_bias_grad,
        conv4_weight_grad,
        conv4_bias_grad,
    )


class Sizes:
    def __init__(self, columns, chan, c_in, c_mid):
        self.columns = columns
        self.frames = columns // AREA
        self.used = self.frames * MAP
        self.pitch = up(self.used, 16)
        self.rows = MAP * self.pitch
        self.padded = self.rows + 2 * self.pitch
        self.chunk = max(n for n in range(16, 129, 16) if self.pitch % n == 0)
        self.c_in, self.c_mid, self.chan = c_in, c_mid, chan
        self.own_in, self.own_mid = c_in // chan, c_mid // chan
        self.groups = ((0, 4), (4, 3), (7, 3), (10, 3))
        self.most = 4 * self.pitch


def up(value, unit):
    return -(-value // unit) * unit


def aligned(value, unit):
    return pl.multiple_of(value, unit)


def column_masks(sizes, width):
    row = lax.broadcasted_iota(jnp.int32, (sizes.pitch, width), 0).astype(F32)
    frame = jnp.floor((row + 0.5) * (1.0 / MAP))
    col = row - frame * MAP
    used = row < sizes.used
    return frame, used, used & (col > 0.5), used & (col < MAP - 1.5)


def loop(count, body):
    def step(index, carry):
        body(index)
        return carry

    lax.fori_loop(0, count, step, 0)


def frame_batches(sizes, move):
    whole = sizes.frames // BATCH

    def body(index):
        move(index * (BATCH * AREA), index * (BATCH * MAP), BATCH)

    if whole:
        loop(whole, body)
    if sizes.frames % BATCH:
        move(whole * BATCH * AREA, whole * BATCH * MAP, sizes.frames % BATCH)


def to_slabs(sizes, flat, slabs, lanes):
    def move(flat_at, slab_at, count):
        source = flat.at[pl.ds(aligned(flat_at, 8), up(count * AREA, 8))]
        for y in range(MAP):
            target = slabs.at[pl.ds(aligned(y * sizes.pitch + slab_at, 8), up(count * MAP, 8))]
            for f in range(count):
                target[f * MAP : (f + 1) * MAP, lanes] = source[f * AREA + y * MAP : f * AREA + (y + 1) * MAP, lanes]

    frame_batches(sizes, move)


def from_slabs(sizes, slabs, flat, lanes):
    def move(flat_at, slab_at, count):
        target = flat.at[pl.ds(aligned(flat_at, 8), up(count * AREA, 8))]
        for y in range(MAP):
            source = slabs.at[pl.ds(aligned(y * sizes.pitch + slab_at, 8), up(count * MAP, 8))]
            for f in range(count):
                target[f * AREA + y * MAP : f * AREA + (y + 1) * MAP, lanes] = source[f * MAP : (f + 1) * MAP, lanes]

    frame_batches(sizes, move)


def turn_in(sizes, field, flat, lanes):
    whole = sizes.columns // WINDOW

    def body(index):
        at = aligned(index * WINDOW, WINDOW)
        flat[pl.ds(at, WINDOW), lanes] = field[:, pl.ds(at, WINDOW)].T.astype(F32)

    loop(whole, body)
    if sizes.columns % WINDOW:
        flat[whole * WINDOW : sizes.columns, lanes] = field[:, whole * WINDOW : sizes.columns].T.astype(F32)


def turn_out(sizes, flat, field, lanes, kind):
    whole = sizes.columns // WINDOW

    def body(index):
        at = aligned(index * WINDOW, WINDOW)
        field[:, pl.ds(at, WINDOW)] = flat[pl.ds(at, WINDOW), lanes].astype(kind).T

    loop(whole, body)
    rest = sizes.columns % WINDOW
    if rest:
        some = up(rest, 16)
        last = flat[whole * WINDOW : whole * WINDOW + some, lanes].astype(kind).T
        field[:, whole * WINDOW : sizes.columns] = last[:, :rest]


def weight_copies(me, weight, kept, sems, half):
    outputs = weight.shape[0]
    copies = []
    for tap in range(9):
        for part in range(2):
            source = aligned(tap * 2 * half + lax.rem(me + part, 2) * half, LANES)
            copies.append(
                pltpu.make_async_copy(
                    weight.at[:, pl.ds(source, half)],
                    kept.at[tap // 3, pl.ds((tap % 3) * outputs, outputs), pl.ds(part * half, half)],
                    sems.at[tap * 2 + part],
                )
            )
    return copies


def conv_terms(sizes, field, kept, first, count, depth, minus, centre, plus):
    span = count * sizes.pitch
    width = kept.shape[1] // 3
    total = None
    for tap_row in range(3):
        rows = field[(first + tap_row) * sizes.pitch : (first + tap_row) * sizes.pitch + span, 0:depth]
        term = lax.dot_general(rows, kept[tap_row], (((1,), (1,)), ((), ())), preferred_element_type=F32)
        total = term if total is None else total + term
    minus[0:8, :] = jnp.zeros((8, width), F32)
    plus[8 + span : 16 + span, :] = jnp.zeros((8, width), F32)
    minus[8 : 8 + span, :] = total[:, 0:width]
    centre[0:span, :] = total[:, width : 2 * width]
    plus[8 : 8 + span, :] = total[:, 2 * width : 3 * width]


def conv_sum(sizes, at, local, minus, centre, plus, left, right):
    n = sizes.chunk
    return (
        centre[pl.ds(at, n), :]
        + minus.at[pl.ds(at, n + 8)][7 : 7 + n, :] * left[pl.ds(local, n), :]
        + plus.at[pl.ds(aligned(at + 8, 8), n + 8)][1 : 1 + n, :] * right[pl.ds(local, n), :]
    )


def each_chunk(sizes, count, body):
    per = sizes.pitch // sizes.chunk

    def step(index):
        body(aligned(index * sizes.chunk, 16), aligned(lax.rem(index, per) * sizes.chunk, 16))

    loop(count * per, step)


def greet(partners):
    barrier = pltpu.get_barrier_semaphore()
    for partner in partners:
        pl.semaphore_signal(barrier, inc=1, device_id=partner, device_id_type=MESH)
    pl.semaphore_wait(barrier, len(partners))


def front_kernel(
    sizes,
    frames_hbm,
    weight_hbm,
    bias,
    cot_hbm,
    field_hbm,
    mid_hbm,
    slope_hbm,
    cot_out_hbm,
    frames,
    cot,
    kept,
    flat,
    slabs,
    field,
    mid,
    slope,
    cot_slabs,
    minus,
    centre,
    plus,
    left,
    right,
    load_sems,
    kept_sems,
    store_sems,
    frame_send,
    frame_recv,
    mid_send,
    mid_recv,
):
    me = lax.axis_index("chan")
    other = (lax.axis_index("dp"), 1 - me)
    own = pltpu.make_async_copy(frames_hbm, frames.at[0], load_sems.at[0])
    own.start()
    greet((other,))
    sent = pltpu.make_async_remote_copy(
        src_ref=frames_hbm,
        dst_ref=frames.at[1],
        send_sem=frame_send,
        recv_sem=frame_recv,
        device_id=other,
        device_id_type=MESH,
    )
    sent.start()
    cot_load = pltpu.make_async_copy(cot_hbm, cot, load_sems.at[1])
    cot_load.start()
    kept_loads = weight_copies(me, weight_hbm, kept, kept_sems, sizes.own_in)
    for copy in kept_loads:
        copy.start()

    _, _, has_left, has_right = column_masks(sizes, sizes.own_mid)
    left[...] = has_left.astype(F32)
    right[...] = has_right.astype(F32)
    field[0 : sizes.pitch, :] = jnp.zeros((sizes.pitch, sizes.c_in), BF16)
    field[sizes.rows + sizes.pitch : sizes.padded, :] = jnp.zeros((sizes.pitch, sizes.c_in), BF16)
    for y in range(MAP):
        end = (y + 1) * sizes.pitch
        slabs[end - 16 : end, :] = jnp.zeros((16, slabs.shape[1]), F32)

    def bring(part, wait):
        lanes = slice(part * sizes.own_in, (part + 1) * sizes.own_in)
        wait()
        turn_in(sizes, frames.at[part], flat, lanes)
        to_slabs(sizes, flat, slabs, lanes)

        def pack(y):
            at = aligned(y * sizes.pitch, 16)
            field[pl.ds(aligned(at + sizes.pitch, 16), sizes.pitch), lanes] = slabs[
                pl.ds(at, sizes.pitch), lanes
            ].astype(BF16)

        loop(MAP, pack)

    bring(0, own.wait)
    bring(1, sent.wait)
    stores = [
        pltpu.make_async_copy(
            field.at[pl.ds(sizes.pitch, sizes.rows)], field_hbm, store_sems.at[0]
        )
    ]
    stores[0].start()
    for copy in kept_loads:
        copy.wait()

    for number, (first, count) in enumerate(sizes.groups):
        conv_terms(sizes, field, kept, first, count, sizes.c_in, minus, centre, plus)
        base = first * sizes.pitch

        def finish(at, local):
            value = conv_sum(sizes, at, local, minus, centre, plus, left, right) + bias[...].astype(F32)
            sigma = 1.0 / (1.0 + jnp.exp(-value))
            rows = pl.ds(aligned(base + at, 16), sizes.chunk)
            mid[rows, :] = (value * sigma).astype(BF16)
            slope[rows, :] = silu_slope(value, sigma)

        each_chunk(sizes, count, finish)
        rows = pl.ds(base, count * sizes.pitch)
        push = pltpu.make_async_remote_copy(
            src_ref=mid.at[rows],
            dst_ref=mid_hbm.at[1, rows],
            send_sem=mid_send.at[number],
            recv_sem=mid_recv.at[number],
            device_id=other,
            device_id_type=MESH,
        )
        keep = pltpu.make_async_copy(mid.at[rows], mid_hbm.at[0, rows], store_sems.at[2 + 2 * number])
        keep_slope = pltpu.make_async_copy(slope.at[rows], slope_hbm.at[rows], store_sems.at[3 + 2 * number])
        for copy in (push, keep, keep_slope):
            copy.start()
            stores.append(copy)

    cot_load.wait()
    turn_in(sizes, cot, flat, slice(0, sizes.own_mid))
    to_slabs(sizes, flat, slabs, slice(0, sizes.own_mid))

    def pack_cot(y):
        at = aligned(y * sizes.pitch, 16)
        cot_slabs[pl.ds(at, sizes.pitch), :] = slabs[pl.ds(at, sizes.pitch), :].astype(BF16)

    loop(MAP, pack_cot)
    stores.append(pltpu.make_async_copy(cot_slabs, cot_out_hbm, store_sems.at[1]))
    stores[-1].start()
    for copy in stores:
        copy.wait()


def front(sizes, frames, weight, bias, cot):
    any_spec = pl.BlockSpec(memory_space=pl.ANY)
    vmem = pl.BlockSpec(memory_space=pltpu.VMEM)
    wide = sizes.own_mid
    groups = len(sizes.groups)
    dma = pltpu.SemaphoreType.DMA
    return pl.pallas_call(
        functools.partial(front_kernel, sizes),
        out_shape=(
            jax.ShapeDtypeStruct((sizes.rows, sizes.c_in), BF16),
            jax.ShapeDtypeStruct((2, sizes.rows, wide), BF16),
            jax.ShapeDtypeStruct((sizes.rows, wide), F32),
            jax.ShapeDtypeStruct((sizes.rows, wide), BF16),
        ),
        in_specs=[any_spec, any_spec, vmem, any_spec],
        out_specs=(any_spec,) * 4,
        scratch_shapes=[
            pltpu.VMEM((2, sizes.own_in, sizes.columns), BF16),
            pltpu.VMEM((wide, sizes.columns), BF16),
            pltpu.VMEM((3, 3 * wide, sizes.c_in), BF16),
            pltpu.VMEM((sizes.rows + 16, wide), F32),
            pltpu.VMEM((sizes.rows, wide), F32),
            pltpu.VMEM((sizes.padded, sizes.c_in), BF16),
            pltpu.VMEM((sizes.rows, wide), BF16),
            pltpu.VMEM((sizes.rows, wide), F32),
            pltpu.VMEM((sizes.rows, wide), BF16),
            pltpu.VMEM((sizes.most + 16, wide), F32),
            pltpu.VMEM((sizes.most, wide), F32),
            pltpu.VMEM((sizes.most + 16, wide), F32),
            pltpu.VMEM((sizes.pitch, wide), F32),
            pltpu.VMEM((sizes.pitch, wide), F32),
            dma((2,)),
            dma((18,)),
            dma((2 + 2 * groups,)),
            dma,
            dma,
            dma((groups,)),
            dma((groups,)),
        ],
        compiler_params=pltpu.CompilerParams(
            collective_id=0, has_side_effects=True, vmem_limit_bytes=60 * MIB
        ),
        cost_estimate=pl.CostEstimate(flops=5 * 10**9, bytes_accessed=2 * 10**7, transcendentals=10**6),
    )(frames, weight, bias, cot)


class Ring:
    def __init__(self, wide_z, wide_y, wide_x):
        dp = lax.axis_index("dp")
        self.me = lax.axis_index("chan")
        self.dp = dp
        self.x = lax.rem(dp, 2)
        self.y = lax.rem(lax.div(dp, 2), 2)
        self.z = lax.div(dp, 4)
        self.core = (dp, 1 - self.me)

    def first(self, kind):
        step = 1 + kind
        side = self.side_first(kind)
        return (self.dp + step * (1 - 2 * side), self.me)

    def second(self, kind):
        step = 2 - kind
        side = self.side_second(kind)
        return (self.dp + step * (1 - 2 * side), self.me)

    def side_first(self, kind):
        return self.x + kind * (self.y - self.x)

    def side_second(self, kind):
        return self.y + kind * (self.x - self.y)

    def along_z(self, hop):
        to = lax.rem(self.z + hop, 4)
        return to, (to * 4 + lax.rem(self.dp, 4), self.me)


def remote(source, target, send, recv, device):
    return pltpu.make_async_remote_copy(
        src_ref=source, dst_ref=target, send_sem=send, recv_sem=recv, device_id=device, device_id_type=MESH
    )


class GradientSum:
    def __init__(self, ring, blocks, done, half_in, quarter_in, piece_in, sems):
        self.ring, self.blocks, self.done = ring, blocks, done
        self.half_in, self.quarter_in, self.piece_in = half_in, quarter_in, piece_in
        (
            self.s1, self.r1, self.s2, self.r2, self.s3, self.r3,
            self.s4, self.r4, self.s5, self.r5, self.s6, self.r6,
        ) = sems
        self.size = blocks.shape[1]

    def half(self, kind, mine):
        side = self.ring.side_first(kind)
        return pl.ds(aligned((side if mine else 1 - side) * (self.size // 2), 16), self.size // 2)

    def quarter(self, kind, mine):
        side = self.ring.side_second(kind)
        at = self.ring.side_first(kind) * (self.size // 2) + (side if mine else 1 - side) * (self.size // 4)
        return pl.ds(aligned(at, 16), self.size // 4)

    def piece(self, kind, z):
        at = (
            self.ring.side_first(kind) * (self.size // 2)
            + self.ring.side_second(kind) * (self.size // 4)
            + z * (self.size // 16)
        )
        return pl.ds(aligned(at, 16), self.size // 16)

    def copy1(self, j, kind):
        return remote(
            self.blocks.at[j, self.half(kind, False)], self.half_in.at[j], self.s1.at[j], self.r1.at[j], self.ring.first(kind)
        )

    def copy2(self, j, kind):
        return remote(
            self.blocks.at[j, self.quarter(kind, False)],
            self.quarter_in.at[j],
            self.s2.at[j],
            self.r2.at[j],
            self.ring.second(kind),
        )

    def copies3(self, j, kind):
        out = []
        for hop in (1, 2, 3):
            to, device = self.ring.along_z(hop)
            out.append(
                remote(
                    self.blocks.at[j, self.piece(kind, to)],
                    self.piece_in.at[j, 3 - hop],
                    self.s3.at[j, hop - 1],
                    self.r3.at[j, 3 - hop],
                    device,
                )
            )
        return out

    def copies4(self, j, kind):
        out = []
        for hop in (1, 2, 3):
            _, device = self.ring.along_z(hop)
            rows = self.done.at[j, self.piece(kind, self.ring.z)]
            out.append(remote(rows, rows, self.s4.at[j, hop - 1], self.r4.at[j, 3 - hop], device))
        return out

    def copy5(self, j, kind):
        rows = self.done.at[j, self.quarter(kind, True)]
        return remote(rows, rows, self.s5.at[j], self.r5.at[j], self.ring.second(kind))

    def copy6(self, j, kind):
        rows = self.done.at[j, self.half(kind, True)]
        return remote(rows, rows, self.s6.at[j], self.r6.at[j], self.ring.first(kind))

    def add(self, j, rows, parts, target):
        total = self.blocks[j, rows, :].astype(F32)
        for part in parts:
            total = total + part.astype(F32)
        target[j, rows, :] = total.astype(BF16)

    def stage1(self, j, kind):
        self.copy1(j, kind).start()

    def stage2(self, j, kind):
        self.copy1(j, kind).wait()
        self.add(j, self.half(kind, True), [self.half_in[j]], self.blocks)
        self.copy2(j, kind).start()

    def stage3(self, j, kind):
        self.copy2(j, kind).wait()
        self.add(j, self.quarter(kind, True), [self.quarter_in[j]], self.blocks)
        for copy in self.copies3(j, kind):
            copy.start()

    def stage4(self, j, kind):
        for copy in self.copies3(j, kind):
            copy.wait()
        self.add(j, self.piece(kind, self.ring.z), [self.piece_in[j, slot] for slot in range(3)], self.done)
        for copy in self.copies4(j, kind):
            copy.start()

    def stage5(self, j, kind):
        for copy in self.copies4(j, kind):
            copy.wait()
        self.copy5(j, kind).start()

    def stage6(self, j, kind):
        self.copy5(j, kind).wait()
        self.copy6(j, kind).start()

    def stage7(self, j, kind):
        self.copy6(j, kind).wait()

    def run(self, stage, first, count):
        step = getattr(self, "stage" + str(stage))

        def body(index):
            j = first + index
            step(j, lax.rem(j, 2))

        loop(count, body)


def back_kernel(
    sizes,
    videos,
    field_hbm,
    mid_hbm,
    slope_hbm,
    cot_hbm,
    weight3_hbm,
    weight4_hbm,
    bias,
    counts,
    conv_hbm,
    frames_grad_hbm,
    grad4_hbm,
    grad3_hbm,
    bias_grads,
    mid,
    shifted4,
    field,
    kept4,
    kept3,
    minus,
    centre,
    plus,
    spread,
    slabs,
    flat,
    outgoing,
    incoming,
    last_out,
    last_in,
    conv_field,
    frames_field,
    left,
    right,
    alive,
    blocks,
    done,
    half_in,
    quarter_in,
    piece_in,
    bias_sum,
    bias_in,
    bias_z,
    mid_sems,
    kept4_sems,
    kept3_sems,
    load_sems,
    out_send,
    out_recv,
    last_send,
    last_recv,
    bias_send,
    bias_recv,
    store_sems,
    block_sems,
    *sum_sems,
):
    ring = Ring(4, 2, 2)
    me = ring.me
    pitch, wide, narrow = sizes.pitch, sizes.own_mid, sizes.own_in
    shifted3 = mid

    mid_loads = []
    for y in range(MAP):
        for part in range(2):
            mid_loads.append(
                pltpu.make_async_copy(
                    mid_hbm.at[part, pl.ds(y * pitch, pitch)],
                    mid.at[pl.ds((y + 1) * pitch, pitch), pl.ds(part * wide, wide)],
                    mid_sems.at[y, part],
                )
            )
    kept4_loads = weight_copies(me, weight4_hbm, kept4, kept4_sems, wide)
    kept3_loads = weight_copies(me, weight3_hbm, kept3, kept3_sems, narrow)
    cot_load = pltpu.make_async_copy(cot_hbm, outgoing, load_sems.at[0])
    slope_load = pltpu.make_async_copy(slope_hbm, flat, load_sems.at[1])
    field_load = pltpu.make_async_copy(field_hbm, field.at[pl.ds(pitch, sizes.rows)], load_sems.at[2])
    lead = 2 * (sizes.groups[0][1] + 1)
    for copy in kept4_loads + mid_loads[:lead] + [cot_load] + mid_loads[lead:] + [slope_load] + kept3_loads + [field_load]:
        copy.start()

    z_devices = [ring.along_z(hop)[1] for hop in (1, 2, 3)]
    greet([ring.core, ring.first(0), ring.first(1)] + z_devices)

    frame, used, has_left, has_right = column_masks(sizes, wide)
    per_video = sizes.frames // videos
    live = None
    for v in range(videos):
        low = v * per_video - 0.5
        inside = (frame > low) & (frame < low + per_video)
        here = inside & (frame < low + counts[v].astype(F32))
        live = here if live is None else live | here
    left[...] = has_left.astype(F32)
    right[...] = has_right.astype(F32)
    alive[...] = (live & used).astype(F32)
    for ref in (mid, shifted4, field):
        blank = jnp.zeros((pitch, ref.shape[1]), BF16)
        ref[0:pitch, :] = blank
        ref[sizes.rows + pitch : sizes.padded, :] = blank
    bias_sum[...] = jnp.zeros(bias_sum.shape, F32)

    def spread_shifted(target, first, count):
        span = count * pitch
        base = (first + 1) * pitch
        spread[0:8, :] = jnp.zeros((8, wide), F32)
        spread[8 + span : 16 + span, :] = jnp.zeros((8, wide), F32)

        def body(at, local):
            n = sizes.chunk
            rows = pl.ds(aligned(base + at, 16), n)
            here = pl.ds(local, n)
            after = spread.at[pl.ds(aligned(at + 8, 8), n + 8)][1 : 1 + n, :] * right[here, :]
            before = spread.at[pl.ds(at, n + 8)][7 : 7 + n, :] * left[here, :]
            target[rows, 0:wide] = after.astype(BF16)
            target[rows, wide : 2 * wide] = spread[pl.ds(aligned(at + 8, 8), n), :].astype(BF16)
            target[rows, 2 * wide : 3 * wide] = before.astype(BF16)

        each_chunk(sizes, count, body)

    def fold(value):
        return jnp.sum(value.reshape(value.shape[0] // 8, 8, value.shape[1]), axis=0)

    for copy in kept4_loads:
        copy.wait()
    for number, (first, count) in enumerate(sizes.groups):
        start = 0 if number == 0 else min(first + 1, MAP)
        for copy in mid_loads[2 * start : 2 * min(first + count + 1, MAP)]:
            copy.wait()
        conv_terms(sizes, mid, kept4, first, count, sizes.c_mid, minus, centre, plus)
        if number == 0:
            cot_load.wait()
        base = first * pitch

        def finish(at, local):
            rows = pl.ds(aligned(base + at, 16), sizes.chunk)
            value = conv_sum(sizes, at, local, minus, centre, plus, left, right) + bias[...].astype(F32)
            sigma = 1.0 / (1.0 + jnp.exp(-value))
            on = alive[pl.ds(local, sizes.chunk), :]
            slabs[rows, :] = on * value * sigma
            grad = (outgoing[rows, :].astype(F32) * on * silu_slope(value, sigma)).astype(BF16).astype(F32)
            spread[pl.ds(aligned(at + 8, 8), sizes.chunk), :] = grad
            bias_sum[:, 0:wide] += fold(grad)

        each_chunk(sizes, count, finish)
        spread_shifted(shifted4, first, count)

    total = GradientSum(ring, blocks, done, half_in, quarter_in, piece_in, sum_sems)
    run = total.run

    def kernel_gradient(grads, values, depth, tap_row, number):
        rows = values[tap_row * pitch : tap_row * pitch + sizes.rows, 0:depth]
        result = lax.dot_general(
            grads[pitch : pitch + sizes.rows, :], rows, (((0,), (0,)), ((), ())), preferred_element_type=F32
        ).astype(BF16)
        for part in range(depth // LANES):
            blocks[number + part] = result[:, part * LANES : (part + 1) * LANES]

    per4, per3 = sizes.c_mid // LANES, sizes.c_in // LANES
    for tap_row in range(3):
        kernel_gradient(shifted4, mid, sizes.c_mid, tap_row, per4 * tap_row)
        run(1, per4 * tap_row, per4)
    run(2, 0, 4)

    for copy in (slope_load,):
        copy.wait()
    stash = (minus, centre)

    def swap4(number):
        first, count = sizes.groups[number]
        rows = pl.ds(first * pitch, count * pitch)
        return remote(outgoing.at[rows], incoming.at[rows], out_send.at[number], out_recv.at[number], ring.core)

    def finish4(number):
        first, count = sizes.groups[number]
        swap4(number).wait()
        base = first * pitch
        own = stash[number % 2]

        def finish(at, local):
            rows = pl.ds(aligned(base + at, 16), sizes.chunk)
            value = own[pl.ds(at, sizes.chunk), :] + incoming[rows, :].astype(F32)
            grad = (value * flat[rows, :]).astype(BF16).astype(F32)
            spread[pl.ds(aligned(at + 8, 8), sizes.chunk), :] = grad
            bias_sum[:, wide : 2 * wide] += fold(grad)

        each_chunk(sizes, count, finish)
        spread_shifted(shifted3, first, count)

    def input_gradient(grads, kept, first, count):
        span = count * pitch
        result = None
        for tap_row in range(3):
            at = (first + 2 - tap_row) * pitch
            term = jnp.dot(grads[at : at + span, :], kept[tap_row], preferred_element_type=F32)
            result = term if result is None else result + term
        return result

    events4 = {0: [(2, 4, 4)], 2: [(2, 8, 4), (3, 0, 4)], 3: [(3, 4, 4)]}
    for number, (first, count) in enumerate(sizes.groups):
        result = input_gradient(shifted4, kept4, first, count)
        span = count * pitch
        stash[number % 2][0:span, :] = result[:, 0:wide]
        outgoing[first * pitch : first * pitch + span, :] = result[:, wide : 2 * wide].astype(BF16)
        swap4(number).start()
        if number:
            finish4(number - 1)
        for event in events4.get(number, ()):
            run(*event)
    finish4(len(sizes.groups) - 1)

    field_load.wait()
    for copy in kept3_loads:
        copy.wait()

    def bias_swap(step):
        device = (ring.first(0), ring.first(1))[step]
        return remote(bias_sum, bias_in.at[step], bias_send.at[step], bias_recv.at[step], device)

    def bias_spread():
        out = []
        for hop in (1, 2, 3):
            _, device = ring.along_z(hop)
            out.append(
                remote(bias_sum, bias_z.at[ring.z], bias_send.at[1 + hop], bias_recv.at[5 - hop], device)
            )
        return out

    bias_swap(0).start()
    events3 = {
        0: [(3, 8, 4), (4, 0, 4)],
        1: [(4, 4, 4)],
        2: [(4, 8, 4), (5, 0, 4)],
    }
    for tap_row in range(3):
        kernel_gradient(shifted3, field, sizes.c_in, tap_row, 3 * per4 + per3 * tap_row)
        run(1, 3 * per4 + per3 * tap_row, per3)
        for event in events3.get(tap_row, ()):
            run(*event)
        if tap_row == 1:
            bias_swap(0).wait()
            bias_sum[...] = bias_sum[...] + bias_in[0]
            bias_swap(1).start()

    from_slabs(sizes, slabs, flat, slice(0, wide))
    turn_out(sizes, flat, conv_field, slice(0, wide), BF16)
    conv_store = pltpu.make_async_copy(conv_field, conv_hbm, store_sems.at[0])
    conv_store.start()

    def swap3(number):
        first, count = sizes.groups[number]
        rows = pl.ds(first * pitch, count * pitch)
        return remote(last_out.at[rows], last_in.at[rows], last_send.at[number], last_recv.at[number], ring.core)

    def finish3(number):
        first, count = sizes.groups[number]
        swap3(number).wait()

        def body(at, _):
            rows = pl.ds(aligned(first * pitch + at, 16), sizes.chunk)
            slabs[rows, 0:narrow] = slabs[rows, 0:narrow] + last_in[rows, :].astype(F32)

        each_chunk(sizes, count, body)

    events_last = {
        0: [(2, 12, 2), (5, 4, 4)],
        1: [(2, 14, 2)],
        2: [(2, 16, 2), (5, 8, 4)],
        3: [(3, 12, 2), (6, 0, 4)],
    }
    for number, (first, count) in enumerate(sizes.groups):
        result = input_gradient(shifted3, kept3, first, count)
        span = count * pitch
        slabs[first * pitch : first * pitch + span, 0:narrow] = result[:, 0:narrow]
        last_out[first * pitch : first * pitch + span, :] = result[:, narrow : 2 * narrow].astype(BF16)
        swap3(number).start()
        if number:
            finish3(number - 1)
        for event in events_last.get(number, ()):
            run(*event)
    finish3(len(sizes.groups) - 1)
    bias_swap(1).wait()
    bias_sum[...] = bias_sum[...] + bias_in[1]
    for copy in bias_spread():
        copy.start()
    run(3, 14, 4)
    run(6, 4, 4)
    from_slabs(sizes, slabs, flat, slice(0, narrow))
    turn_out(sizes, flat, frames_field, slice(0, narrow), F32)
    frames_store = pltpu.make_async_copy(frames_field, frames_grad_hbm, store_sems.at[1])
    frames_store.start()
    run(4, 12, 6)
    run(6, 8, 4)

    def block_stores(j, grad_hbm, tap_row, part, parts):
        out = []
        column_block = lax.rem(part + me * (parts // 2), parts)
        for tap_col in range(3):
            at = aligned(((tap_row * 3 + tap_col) * parts + column_block) * LANES, LANES)
            out.append(
                pltpu.make_async_copy(
                    done.at[j, pl.ds(tap_col * wide, wide)],
                    grad_hbm.at[:, pl.ds(at, LANES)],
                    block_sems.at[j, tap_col],
                )
            )
        return out

    def stores4(j):
        return block_stores(j, grad4_hbm, lax.div(j, per4), lax.rem(j, per4), per4)

    def stores3(j):
        at = j - 3 * per4
        return block_stores(j, grad3_hbm, lax.div(at, per3), lax.rem(at, per3), per3)

    def start_all(stores, first):
        def body(index):
            for copy in stores(first + index):
                copy.start()

        return body

    def wait_all(stores, first):
        def body(index):
            for copy in stores(first + index):
                copy.wait()

        return body

    run(7, 0, 4)
    loop(4, start_all(stores4, 0))
    run(5, 12, 6)
    run(7, 4, 8)
    loop(2 * per4, start_all(stores4, 4))
    for copy in bias_spread():
        copy.wait()
    bias_z[ring.z] = bias_sum[...]
    summed = bias_z[0] + bias_z[1] + bias_z[2] + bias_z[3]
    bias_grads[...] = jnp.sum(summed, axis=0, keepdims=True)
    run(6, 12, 6)
    run(7, 12, 6)
    loop(3 * per3, start_all(stores3, 3 * per4))
    conv_store.wait()
    frames_store.wait()
    loop(3 * per4, wait_all(stores4, 0))
    loop(3 * per3, wait_all(stores3, 3 * per4))


def back(sizes, videos, field, mid, slope, cot, weight3, weight4, bias, counts):
    any_spec = pl.BlockSpec(memory_space=pl.ANY)
    vmem = pl.BlockSpec(memory_space=pltpu.VMEM)
    smem = pl.BlockSpec(memory_space=pltpu.SMEM)
    wide, narrow, pitch = sizes.own_mid, sizes.own_in, sizes.pitch
    groups = len(sizes.groups)
    dma = pltpu.SemaphoreType.DMA
    count = 3 * (sizes.c_mid + sizes.c_in) // LANES
    tall = 3 * wide
    ones, threes = [dma((count,))] * 2, [dma((count, 3))] * 2
    return pl.pallas_call(
        functools.partial(back_kernel, sizes, videos),
        out_shape=(
            jax.ShapeDtypeStruct((wide, sizes.columns), BF16),
            jax.ShapeDtypeStruct((narrow, sizes.columns), F32),
            jax.ShapeDtypeStruct((wide, 9 * sizes.c_mid), BF16),
            jax.ShapeDtypeStruct((wide, 9 * sizes.c_in), BF16),
            jax.ShapeDtypeStruct((1, 2 * wide), F32),
        ),
        in_specs=[any_spec] * 6 + [vmem, smem],
        out_specs=(any_spec,) * 4 + (vmem,),
        scratch_shapes=[
            pltpu.VMEM((sizes.padded, tall), BF16),
            pltpu.VMEM((sizes.padded, tall), BF16),
            pltpu.VMEM((sizes.padded, sizes.c_in), BF16),
            pltpu.VMEM((3, tall, sizes.c_mid), BF16),
            pltpu.VMEM((3, tall, sizes.c_in), BF16),
            pltpu.VMEM((sizes.most + 16, wide), F32),
            pltpu.VMEM((sizes.most, wide), F32),
            pltpu.VMEM((sizes.most + 16, wide), F32),
            pltpu.VMEM((sizes.most + 16, wide), F32),
            pltpu.VMEM((sizes.rows, wide), F32),
            pltpu.VMEM((sizes.rows, wide), F32),
            pltpu.VMEM((sizes.rows, wide), BF16),
            pltpu.VMEM((sizes.rows, wide), BF16),
            pltpu.VMEM((sizes.rows, narrow), BF16),
            pltpu.VMEM((sizes.rows, narrow), BF16),
            pltpu.VMEM((wide, sizes.columns), BF16),
            pltpu.VMEM((narrow, sizes.columns), F32),
            pltpu.VMEM((pitch, wide), F32),
            pltpu.VMEM((pitch, wide), F32),
            pltpu.VMEM((pitch, wide), F32),
            pltpu.VMEM((count, tall, LANES), BF16),
            pltpu.VMEM((count, tall, LANES), BF16),
            pltpu.VMEM((count, tall // 2, LANES), BF16),
            pltpu.VMEM((count, tall // 4, LANES), BF16),
            pltpu.VMEM((count, 3, tall // 16, LANES), BF16),
            pltpu.VMEM((8, 2 * wide), F32),
            pltpu.VMEM((2, 8, 2 * wide), F32),
            pltpu.VMEM((4, 8, 2 * wide), F32),
            dma((MAP, 2)),
            dma((18,)),
            dma((18,)),
            dma((3,)),
            dma((groups,)),
            dma((groups,)),
            dma((groups,)),
            dma((groups,)),
            dma((5,)),
            dma((5,)),
            dma((2,)),
            dma((count, 3)),
        ]
        + ones + ones + threes + threes + ones + ones,
        compiler_params=pltpu.CompilerParams(
            collective_id=1, has_side_effects=True, vmem_limit_bytes=63 * MIB
        ),
        cost_estimate=pl.CostEstimate(flops=4 * 10**10, bytes_accessed=4 * 10**7, transcendentals=10**6),
    )(field, mid, slope, cot, weight3, weight4, bias, counts)


def kernel_device(frames, clip_counts, conv3_weight, conv3_bias, conv4_weight, conv4_bias, cotangent):
    wide = conv3_weight.shape[0]
    sizes = Sizes(frames.shape[1], 2, conv3_weight.shape[1] // 9, conv4_weight.shape[1] // 9)
    field, mid, slope, cot = front(sizes, frames, conv3_weight, conv3_bias.reshape(1, -1), cotangent)
    conv4_out, frames_grad, grad4, grad3, biases = back(
        sizes,
        clip_counts.shape[0],
        field,
        mid,
        slope,
        cot,
        conv3_weight,
        conv4_weight,
        conv4_bias.reshape(1, -1),
        clip_counts,
    )
    return (
        conv4_out,
        frames_grad,
        grad3.astype(F32),
        biases[0, wide:],
        grad4.astype(F32),
        biases[0, :wide],
    )


def solution(mesh):
    in_specs = (
        P("chan", "dp"),
        P("dp"),
        P("chan", None),
        P("chan"),
        P("chan", None),
        P("chan"),
        P("chan", "dp"),
    )
    out_specs = (
        P("chan", "dp"),
        P("chan", "dp"),
        P("chan", None),
        P("chan"),
        P("chan", None),
        P("chan"),
    )
    fits = mesh.shape["chan"] == 2 and mesh.shape["dp"] == 16
    per_device = kernel_device if fits else general_device
    return jax.shard_map(
        per_device, mesh=mesh, in_specs=in_specs, out_specs=out_specs, check_vma=False
    )
```

```python
import functools

import jax
import jax.numpy as jnp
from jax import lax
from jax.experimental import pallas as pl
from jax.experimental.pallas import tpu as pltpu
from jax.sharding import PartitionSpec as P

MAP = 13
AREA = MAP * MAP
LANES = 128
WINDOW = 256
BATCH = 8
MESH = pl.DeviceIdType.MESH
F32 = jnp.float32
BF16 = jnp.bfloat16
MIB = 2**20


def shift_cols(values, offset):
    if offset == 0:
        return values
    if offset > 0:
        return jnp.pad(values[:, offset:], ((0, 0), (0, offset)))
    return jnp.pad(values[:, :offset], ((0, 0), (-offset, 0)))


def tap_table(count):
    pixel = jnp.arange(count, dtype=jnp.int32) % AREA
    row_of = pixel // MAP
    col_of = pixel % MAP
    table = []
    for tap in range(9):
        tap_row = tap // 3
        tap_col = tap % 3
        src_row = row_of + tap_row - 1
        src_col = col_of + tap_col - 1
        valid = (src_row >= 0) & (src_row < MAP) & (src_col >= 0) & (src_col < MAP)
        table.append(((tap_row - 1) * MAP + tap_col - 1, valid[None, :]))
    return table


def conv_forward(field, kernel, table):
    result = None
    for tap in range(9):
        offset, valid = table[tap]
        term = jnp.dot(kernel[:, tap, :], field, preferred_element_type=F32)
        term = jnp.where(valid, shift_cols(term, offset), 0.0)
        result = term if result is None else result + term
    return result


def conv_backward(grad_field, kernel, table):
    result = None
    for tap in range(9):
        offset, valid = table[tap]
        masked = jnp.where(valid, grad_field, jnp.zeros((), grad_field.dtype))
        moved = shift_cols(masked, -offset)
        term = jnp.einsum("dc,dp->cp", kernel[:, tap, :], moved, preferred_element_type=F32)
        result = term if result is None else result + term
    return result


def kernel_grad(field, grad_field, table):
    taps_out = []
    for tap in range(9):
        offset, valid = table[tap]
        masked = jnp.where(valid, grad_field, jnp.zeros((), grad_field.dtype))
        moved = shift_cols(masked, -offset)
        taps_out.append(jnp.einsum("dp,cp->dc", moved, field, preferred_element_type=F32))
    return jnp.concatenate(taps_out, axis=1)


def silu_slope(value, sigma):
    return sigma * (1.0 + value * (1.0 - sigma))


def unpack(flat, shapes):
    pieces = []
    offset = 0
    for shape in shapes:
        length = 1
        for extent in shape:
            length = length * extent
        pieces.append(flat[offset : offset + length].reshape(shape))
        offset = offset + length
    return pieces


def general_device(frames, clip_counts, conv3_weight, conv3_bias, conv4_weight, conv4_bias, cotangent):
    columns = frames.shape[1]
    frame_count = columns // AREA
    videos_here = clip_counts.shape[0]
    per_video = frame_count // videos_here
    out_width = conv3_weight.shape[0]
    frame_ids = jnp.arange(frame_count, dtype=jnp.int32)
    owner = (frame_ids // per_video)[:, None] == jnp.arange(videos_here, dtype=jnp.int32)[None, :]
    count_of = jnp.sum(jnp.where(owner, clip_counts[None, :], 0), axis=1)
    frame_alive = (frame_ids % per_video < count_of).astype(F32)
    alive = jnp.broadcast_to(frame_alive[:, None], (frame_count, AREA)).reshape(1, columns)
    table = tap_table(columns)
    kernel3 = conv3_weight.reshape(out_width, 9, -1)
    kernel4 = conv4_weight.reshape(out_width, 9, -1)
    full_input = lax.all_gather(frames, "chan", axis=0, tiled=True)
    pre3 = conv_forward(full_input, kernel3, table) + conv3_bias.astype(F32)[:, None]
    sigma3 = jax.nn.sigmoid(pre3)
    mid = (pre3 * sigma3).astype(BF16)
    full_mid = lax.all_gather(mid, "chan", axis=0, tiled=True)
    pre4 = conv_forward(full_mid, kernel4, table) + conv4_bias.astype(F32)[:, None]
    sigma4 = jax.nn.sigmoid(pre4)
    conv4_out = (alive * pre4 * sigma4).astype(BF16)
    grad4 = (cotangent.astype(F32) * alive * silu_slope(pre4, sigma4)).astype(BF16)
    kernel4_local = kernel_grad(full_mid, grad4, table)
    bias4_local = jnp.sum(grad4.astype(F32), axis=1)
    shapes4 = (kernel4_local.shape, bias4_local.shape)
    partial_terms = conv_backward(grad4, kernel4, table)
    grad_mid = lax.psum_scatter(partial_terms, "chan", scatter_dimension=0, tiled=True)
    grad3 = (grad_mid * silu_slope(pre3, sigma3)).astype(BF16)
    kernel3_local = kernel_grad(full_input, grad3, table)
    bias3_local = jnp.sum(grad3.astype(F32), axis=1)
    shapes3 = (kernel3_local.shape, bias3_local.shape)
    input_terms = conv_backward(grad3, kernel3, table)
    frames_grad = lax.psum_scatter(input_terms, "chan", scatter_dimension=0, tiled=True)
    packed = jnp.concatenate(
        [item.reshape(-1) for item in (kernel3_local, bias3_local, kernel4_local, bias4_local)]
    )
    whole = lax.psum(packed, "dp")
    conv3_weight_grad, conv3_bias_grad, conv4_weight_grad, conv4_bias_grad = unpack(
        whole, shapes3 + shapes4
    )
    return (
        conv4_out,
        frames_grad,
        conv3_weight_grad,
        conv3_bias_grad,
        conv4_weight_grad,
        conv4_bias_grad,
    )


def up(value, unit):
    return -(-value // unit) * unit


def aligned(value, unit):
    return pl.multiple_of(value, unit)


class Sizes:
    def __init__(self, columns, chan, c_in, c_mid):
        self.columns = columns
        self.frames = columns // AREA
        self.used = self.frames * MAP
        self.pitch = up(self.used, 16)
        self.rows = MAP * self.pitch
        self.c_in, self.c_mid = c_in, c_mid
        self.own_in, self.own_mid = c_in // chan, c_mid // chan
        self.tall = 3 * self.own_mid
        self.blocks4, self.blocks3 = 3 * c_mid // LANES, 3 * c_in // LANES
        self.blocks = self.blocks4 + self.blocks3

    def slab(self, y):
        return slice(y * self.pitch, (y + 1) * self.pitch)


def column_masks(sizes, width):
    row = lax.broadcasted_iota(jnp.int32, (sizes.pitch, width), 0).astype(F32)
    frame = jnp.floor((row + 0.5) * (1.0 / MAP))
    col = row - frame * MAP
    used = row < sizes.used
    return frame, used, used & (col > 0.5), used & (col < MAP - 1.5)


def loop(count, body):
    def step(index, carry):
        body(index)
        return carry

    lax.fori_loop(0, count, step, 0)


def frame_batches(sizes, flat, slabs, move):
    whole = sizes.frames // BATCH

    def body(index):
        part = flat.at[pl.ds(aligned(index * (BATCH * AREA), 8), BATCH * AREA)]
        at = index * (BATCH * MAP)
        rows = [slabs.at[pl.ds(aligned(y * sizes.pitch + at, 8), BATCH * MAP)] for y in range(MAP)]
        for f in range(BATCH):
            for y in range(MAP):
                move(part, f * AREA + y * MAP, rows[y], f * MAP)

    if whole:
        loop(whole, body)
    for f in range(whole * BATCH, sizes.frames):
        for y in range(MAP):
            move(flat, f * AREA + y * MAP, slabs, y * sizes.pitch + f * MAP)


def to_slabs(sizes, flat, slabs, lanes):
    def move(source, source_at, target, target_at):
        target[target_at : target_at + MAP, lanes] = source[source_at : source_at + MAP, lanes]

    frame_batches(sizes, flat, slabs, move)


def from_slabs(sizes, slabs, flat, lanes):
    def move(target, target_at, source, source_at):
        target[target_at : target_at + MAP, :] = source[source_at : source_at + MAP, lanes]

    frame_batches(sizes, flat, slabs, move)


def windows(sizes, move):
    whole = sizes.columns // WINDOW
    loop(whole, lambda index: move(pl.ds(aligned(index * WINDOW, WINDOW), WINDOW)))
    if sizes.columns % WINDOW:
        move(slice(whole * WINDOW, sizes.columns))


def remote(source, target, send, recv, device):
    return pltpu.make_async_remote_copy(
        src_ref=source, dst_ref=target, send_sem=send, recv_sem=recv, device_id=device, device_id_type=MESH
    )


def weight_copies(me, weight, kept, sems, half):
    outputs = weight.shape[0]
    copies = []
    for tap in range(9):
        for part in range(2):
            source = aligned(tap * 2 * half + lax.rem(me + part, 2) * half, LANES)
            copies.append(
                pltpu.make_async_copy(
                    weight.at[:, pl.ds(source, half)],
                    kept.at[tap // 3, pl.ds((tap % 3) * outputs, outputs), pl.ds(part * half, half)],
                    sems.at[tap * 2 + part],
                )
            )
    return copies


def conv_terms(sizes, field, kept, y, depth):
    rows = [r for r in range(3) if 0 <= y + r - 1 < MAP]
    taps = jnp.concatenate([field[sizes.slab(y + r - 1), 0:depth] for r in rows], axis=1)
    width = kept.shape[1] // 3
    out = []
    for s in range(3):
        weights = jnp.concatenate([kept[r, s * width : (s + 1) * width, :] for r in rows], axis=1)
        out.append(lax.dot_general(taps, weights, (((1,), (1,)), ((), ())), preferred_element_type=F32))
    return out


def input_gradient(sizes, grads, kept, y):
    rows = [r for r in range(3) if 0 <= y + 1 - r < MAP]
    taps = jnp.concatenate([grads[sizes.slab(y + 1 - r), :] for r in rows], axis=1)
    weights = jnp.concatenate([kept[r] for r in rows], axis=0)
    return jnp.dot(taps, weights, preferred_element_type=F32)


def kernel_gradient(sizes, grads, values, r, lanes):
    span = sizes.rows - (sizes.pitch if r != 1 else 0)
    at = sizes.pitch if r == 0 else 0
    to = sizes.pitch if r == 2 else 0
    return lax.dot_general(
        grads[at : at + span, :], values[to : to + span, lanes], (((0,), (0,)), ((), ())), preferred_element_type=F32
    )


def before(value):
    return pltpu.roll(value, 1, 0)


def after(value):
    return pltpu.roll(value, value.shape[0] - 1, 0)


def sigmoid(value):
    return 1.0 / (1.0 + jnp.exp(-value))


def fold(value):
    return jnp.sum(value.reshape(value.shape[0] // 8, 8, value.shape[1]), axis=0)


class Ring:
    def __init__(self):
        self.dp = lax.axis_index("dp")
        self.me = lax.axis_index("chan")
        self.bits = [lax.rem(lax.div(self.dp, 2**bit), 2) for bit in range(4)]
        self.core = (self.dp, 1 - self.me)

    def across(self, bit):
        return (self.dp + 2**bit * (1 - 2 * self.bits[bit]), self.me)

    def side(self, step, kind):
        x, y, low, high = self.bits
        return (x + kind * (y - x), low, y + kind * (x - y), high)[step]

    def partner(self, step, kind):
        apart = (1 + kind, 4, 2 - kind, 8)[step]
        return (self.dp + apart * (1 - 2 * self.side(step, kind)), self.me)


class GradientSum:
    def __init__(self, ring, keep, outs, ins, done, sends, recvs):
        self.ring, self.keep, self.outs, self.ins, self.done = ring, keep, outs, ins, done
        self.sends, self.recvs = sends, recvs
        self.size = done.shape[1]

    def kept(self, step, kind, mine):
        at = 0
        for s in range(1, step + 1):
            side = self.ring.side(s, kind)
            at = at + (side if mine or s < step else 1 - side) * (self.size >> (s + 1))
        return pl.ds(aligned(at, 16), self.size >> (step + 1))

    def finished(self, step, kind):
        at = 0
        for s in range(step + 1):
            at = at + self.ring.side(s, kind) * (self.size >> (s + 1))
        return pl.ds(aligned(at, 16), self.size >> (step + 1))

    def down(self, step, j, kind):
        return remote(
            self.outs[step].at[j],
            self.ins[step].at[j],
            self.sends[step].at[j],
            self.recvs[step].at[j],
            self.ring.partner(step, kind),
        )

    def back(self, step, j, kind):
        rows = self.done.at[j, self.finished(step, kind)]
        return remote(rows, rows, self.sends[7 - step].at[j], self.recvs[7 - step].at[j], self.ring.partner(step, kind))

    def stage(self, number, j, kind):
        if number == 0:
            self.down(0, j, kind).start()
        elif number < 4:
            self.down(number - 1, j, kind).wait()
            rows = self.kept(number - 1, kind, True) if number > 1 else slice(None)
            self.keep[j, rows, :] = self.keep[j, rows, :] + self.ins[number - 1][j].astype(F32)
            self.outs[number][j] = self.keep[j, self.kept(number, kind, False), :].astype(BF16)
            self.down(number, j, kind).start()
        elif number == 4:
            self.down(3, j, kind).wait()
            total = self.keep[j, self.kept(3, kind, True), :] + self.ins[3][j].astype(F32)
            self.done[j, self.finished(3, kind), :] = total.astype(BF16)
            self.back(3, j, kind).start()
        else:
            self.back(8 - number, j, kind).wait()
            if number < 8:
                self.back(7 - number, j, kind).start()

    def run(self, number, first, count):
        def body(index):
            j = first + index
            self.stage(number, j, lax.rem(j, 2))

        loop(count, body)


def net_kernel(
    sizes,
    videos,
    frames_hbm,
    cot_hbm,
    weight3_hbm,
    weight4_hbm,
    bias3,
    bias4,
    counts,
    conv_hbm,
    frames_grad_hbm,
    grad4_hbm,
    grad3_hbm,
    bias_grads,
    frames,
    cot,
    kept3,
    kept4,
    flat,
    slabs,
    field,
    mid,
    shifted4,
    outgoing,
    incoming,
    last_in,
    frames_field,
    left,
    right,
    alive,
    stash,
    result,
    bias_sum,
    bias_in,
    keep,
    done,
    out0,
    out1,
    out2,
    out3,
    in0,
    in1,
    in2,
    in3,
    load_sems,
    kept3_sems,
    kept4_sems,
    frame_sems,
    mid_send,
    mid_recv,
    out_send,
    out_recv,
    last_send,
    last_recv,
    bias_send,
    bias_recv,
    store_sems,
    block_sems,
    *sum_sems,
):
    ring = Ring()
    me = ring.me
    pitch, wide, narrow = sizes.pitch, sizes.own_mid, sizes.own_in
    slab = sizes.slab
    shifted3 = mid

    own_load = pltpu.make_async_copy(frames_hbm, frames.at[0], load_sems.at[0])
    cot_load = pltpu.make_async_copy(cot_hbm, cot, load_sems.at[1])
    kept3_loads = weight_copies(me, weight3_hbm, kept3, kept3_sems, narrow)
    kept4_loads = weight_copies(me, weight4_hbm, kept4, kept4_sems, wide)
    own_load.start()

    barrier = pltpu.get_barrier_semaphore()
    partners = [ring.core] + [ring.across(bit) for bit in range(4)]
    for partner in partners:
        pl.semaphore_signal(barrier, inc=1, device_id=partner, device_id_type=MESH)
    pl.semaphore_wait(barrier, len(partners))

    swap_frames = remote(frames_hbm, frames.at[1], frame_sems.at[0], frame_sems.at[1], ring.core)
    swap_frames.start()
    for copy in [cot_load] + kept3_loads + kept4_loads:
        copy.start()

    frame, used, has_left, has_right = column_masks(sizes, wide)
    per_video = sizes.frames // videos
    live = None
    for v in range(videos):
        low = v * per_video - 0.5
        here = (frame > low) & (frame < low + per_video) & (frame < low + counts[v].astype(F32))
        live = here if live is None else live | here
    left[...] = has_left.astype(F32)
    right[...] = has_right.astype(F32)
    alive[...] = (live & used).astype(F32)
    bias_sum[...] = jnp.zeros(bias_sum.shape, F32)
    for y in range(MAP):
        slabs[(y + 1) * pitch - 16 : (y + 1) * pitch, :] = jnp.zeros((16, wide), F32)

    def bring(source, lanes, target):
        def widen(rows):
            flat[rows, lanes] = source[rows, :].astype(F32)

        windows(sizes, widen)
        to_slabs(sizes, flat, slabs, lanes)

        def pack(y):
            rows = pl.ds(aligned(y * pitch, 16), pitch)
            target[rows, lanes] = slabs[rows, lanes].astype(BF16)

        loop(MAP, pack)

    own_load.wait()
    bring(frames.at[0], slice(0, narrow), field)
    cot_load.wait()
    bring(cot, slice(0, wide), outgoing)
    swap_frames.wait()
    bring(frames.at[1], slice(narrow, 2 * narrow), field)
    for copy in kept3_loads:
        copy.wait()

    def swap_mid(y):
        return remote(
            mid.at[slab(y), 0:wide], mid.at[slab(y), wide : 2 * wide], mid_send.at[y], mid_recv.at[y], ring.core
        )

    def joined(terms, bias):
        minus, centre, plus = terms
        return centre + before(minus) * left[...] + after(plus) * right[...] + bias[...].astype(F32).reshape(1, -1)

    def finish3(y, terms):
        value = joined(terms, bias3)
        sigma = sigmoid(value)
        mid[slab(y), 0:wide] = (value * sigma).astype(BF16)
        flat[slab(y), :] = silu_slope(value, sigma)
        swap_mid(y).start()

    waiting = None
    for y in range(MAP):
        terms = conv_terms(sizes, field, kept3, y, sizes.c_in)
        if waiting is not None:
            finish3(*waiting)
        waiting = (y, terms)
    finish3(*waiting)

    def shift_out(target, y, rounded):
        grad = rounded.astype(F32)
        target[slab(y), 0:wide] = (after(grad) * right[...]).astype(BF16)
        target[slab(y), wide : 2 * wide] = rounded
        target[slab(y), 2 * wide : 3 * wide] = (before(grad) * left[...]).astype(BF16)
        return fold(grad)

    def finish4(y, terms):
        value = joined(terms, bias4)
        sigma = sigmoid(value)
        on = alive[...]
        slabs[slab(y), :] = on * value * sigma
        return shift_out(
            shifted4, y, (outgoing[slab(y), :].astype(F32) * on * silu_slope(value, sigma)).astype(BF16)
        )

    for copy in kept4_loads:
        copy.wait()
    middle = MAP // 2
    summed = jnp.zeros((8, wide), F32)
    waiting = None
    for y in range(MAP):
        if y == 0:
            for other in range(middle + 1):
                swap_mid(other).wait()
        if y == middle:
            for other in range(middle + 1, MAP):
                swap_mid(other).wait()
        terms = conv_terms(sizes, mid, kept4, y, sizes.c_mid)
        if waiting is not None:
            summed = summed + finish4(*waiting)
        waiting = (y, terms)
    bias_sum[:, 0:wide] = summed + finish4(*waiting)

    total = GradientSum(
        ring, keep, (out0, out1, out2, out3), (in0, in1, in2, in3), done, sum_sems[:8], sum_sems[8:]
    )
    run = total.run
    half = sizes.tall // 2

    def give(value, number):
        result[...] = value
        for part in range(2):
            side = ring.side(0, (number + part) % 2)
            lanes = slice(part * LANES, (part + 1) * LANES)
            keep[number + part] = result[pl.ds(aligned(side * half, 16), half), lanes]
            out0[number + part] = result[pl.ds(aligned((1 - side) * half, 16), half), lanes].astype(BF16)
            total.stage(0, number + part, (number + part) % 2)

    step = 0
    events = EVENTS["kernel4"]
    for r in range(3):
        for part in range(sizes.c_mid // WINDOW):
            lanes = slice(part * WINDOW, (part + 1) * WINDOW)
            give(kernel_gradient(sizes, shifted4, mid, r, lanes), 2 * step)
            for event in events.get(step, ()):
                run(*event)
            step += 1

    def swap4(y):
        return remote(outgoing.at[slab(y)], incoming.at[slab(y)], out_send.at[y], out_recv.at[y], ring.core)

    def finish_back(y):
        value = stash[y % 4] + incoming[slab(y), :].astype(F32)
        return shift_out(shifted3, y, (value * flat[slab(y), :]).astype(BF16))

    summed = jnp.zeros((8, wide), F32)
    events = EVENTS["input4"]
    for y in range(MAP + LAG):
        if y >= LAG:
            swap4(y - LAG).wait()
        if y < MAP:
            grad = input_gradient(sizes, shifted4, kept4, y)
            stash[y % 4] = grad[:, 0:wide]
            outgoing[slab(y), :] = grad[:, wide : 2 * wide].astype(BF16)
        if y >= LAG:
            summed = summed + finish_back(y - LAG)
        if y < MAP:
            swap4(y).start()
        for event in events.get(y, ()):
            run(*event)
    bias_sum[:, wide : 2 * wide] = summed

    def swap_bias(bit):
        return remote(bias_sum, bias_in.at[bit], bias_send.at[bit], bias_recv.at[bit], ring.across(bit))

    def add_bias(bit):
        swap_bias(bit).wait()
        bias_sum[...] = bias_sum[...] + bias_in[bit]

    events = EVENTS["kernel3"]
    for r in range(3):
        give(kernel_gradient(sizes, shifted3, field, r, slice(0, sizes.c_in)), 2 * step)
        for event in events.get(r, ()):
            run(*event)
        step += 1

    swap_bias(0).start()
    from_slabs(sizes, slabs, flat, slice(0, wide))

    def narrow_down(rows):
        cot[rows, :] = flat[rows, :].astype(BF16)

    windows(sizes, narrow_down)
    conv_store = pltpu.make_async_copy(cot, conv_hbm, store_sems.at[0])
    conv_store.start()
    for event in EVENTS["between"]:
        run(*event)

    def swap3(y):
        return remote(
            outgoing.at[slab(y), 0:narrow], last_in.at[slab(y)], last_send.at[y], last_recv.at[y], ring.core
        )

    events = EVENTS["input3"]
    for y in range(MAP):
        grad = input_gradient(sizes, shifted3, kept3, y)
        slabs[slab(y), 0:narrow] = grad[:, 0:narrow]
        outgoing[slab(y), 0:narrow] = grad[:, narrow : 2 * narrow].astype(BF16)
        swap3(y).start()
        for event in events.get(y, ()):
            run(*event)
    add_bias(0)
    swap_bias(1).start()
    for y in range(MAP):
        swap3(y).wait()

    def join(y):
        rows = pl.ds(aligned(y * pitch, 16), pitch)
        slabs[rows, 0:narrow] = slabs[rows, 0:narrow] + last_in[rows, :].astype(F32)

    loop(MAP, join)
    from_slabs(sizes, slabs, frames_field, slice(0, narrow))
    frames_store = pltpu.make_async_copy(frames_field, frames_grad_hbm, store_sems.at[1])
    frames_store.start()
    add_bias(1)
    swap_bias(2).start()

    def block_stores(j, grad_hbm, first, parts):
        r, part = lax.div(j - first, parts), lax.rem(j - first, parts)
        column_block = lax.rem(part + me * (parts // 2), parts)
        out = []
        for s in range(3):
            at = aligned(((r * 3 + s) * parts + column_block) * LANES, LANES)
            out.append(
                pltpu.make_async_copy(
                    done.at[j, pl.ds(s * wide, wide)], grad_hbm.at[:, pl.ds(at, LANES)], block_sems.at[j, s]
                )
            )
        return out

    def stores4(j):
        return block_stores(j, grad4_hbm, 0, sizes.c_mid // LANES)

    def stores3(j):
        return block_stores(j, grad3_hbm, sizes.blocks4, sizes.c_in // LANES)

    def save(stores, first, count):
        def body(index):
            j = first + index
            total.stage(8, j, lax.rem(j, 2))
            for copy in stores(j):
                copy.start()

        loop(count, body)

    def saved(stores, first, count):
        def body(index):
            for copy in stores(first + index):
                copy.wait()

        loop(count, body)

    for event in EVENTS["last"]:
        if event[0] == "bias":
            add_bias(event[1])
            if event[1] < 3:
                swap_bias(event[1] + 1).start()
        elif event[0] == 8:
            save(stores4 if event[1] < sizes.blocks4 else stores3, event[1], event[2])
        else:
            run(*event)
    bias_grads[...] = jnp.sum(bias_sum[...], axis=0, keepdims=True)
    conv_store.wait()
    frames_store.wait()
    saved(stores4, 0, sizes.blocks4)
    saved(stores3, sizes.blocks4, sizes.blocks3)


LAG = 3
EVENTS = {
    "kernel4": {4: [(1, 0, 2)], 5: [(1, 2, 2)]},
    "input4": {
        0: [(1, 4, 2)],
        2: [(1, 6, 2)],
        4: [(2, 0, 2)],
        5: [(1, 8, 2), (2, 2, 2)],
        6: [(2, 4, 2)],
        8: [(1, 10, 2), (2, 6, 2)],
        9: [(3, 0, 2)],
        10: [(3, 2, 2), (2, 8, 2)],
        11: [(3, 4, 2)],
        12: [(4, 0, 2)],
        13: [(2, 10, 2), (3, 6, 2)],
        14: [(4, 2, 2)],
        15: [(5, 0, 2), (4, 4, 2)],
    },
    "kernel3": {
        0: [(3, 8, 2), (4, 6, 2), (5, 2, 2)],
        1: [(3, 10, 2), (4, 8, 2), (6, 0, 4), (5, 4, 4)],
        2: [(4, 10, 2), (5, 8, 2), (7, 0, 2), (6, 4, 4)],
    },
    "between": [(7, 2, 4), (5, 10, 2), (6, 8, 2), (1, 12, 2)],
    "input3": {
        2: [(7, 6, 2), (1, 14, 2)],
        4: [(6, 10, 2), (7, 8, 2)],
        6: [(1, 16, 2)],
        8: [(2, 12, 2)],
        10: [(7, 10, 2), (2, 14, 2)],
    },
    "last": [
        (2, 16, 2), (3, 12, 2), (8, 0, 4), (3, 14, 2), ("bias", 2), (4, 12, 2), (3, 16, 2), (4, 14, 2), (8, 4, 4),
        (5, 12, 2), (4, 16, 2), (5, 14, 2), ("bias", 3), (6, 12, 2), (5, 16, 2), (6, 14, 2), (7, 12, 2), (6, 16, 2),
        (7, 14, 2), (7, 16, 2), (8, 8, 4), (8, 12, 6),
    ],
}


def net(sizes, videos, frames, cot, weight3, weight4, bias3, bias4, counts):
    any_spec = pl.BlockSpec(memory_space=pl.ANY)
    vmem = pl.BlockSpec(memory_space=pltpu.VMEM)
    smem = pl.BlockSpec(memory_space=pltpu.SMEM)
    wide, narrow, pitch, rows, tall = sizes.own_mid, sizes.own_in, sizes.pitch, sizes.rows, sizes.tall
    blocks = sizes.blocks
    dma = pltpu.SemaphoreType.DMA
    return pl.pallas_call(
        functools.partial(net_kernel, sizes, videos),
        out_shape=(
            jax.ShapeDtypeStruct((sizes.columns, wide), BF16),
            jax.ShapeDtypeStruct((sizes.columns, narrow), F32),
            jax.ShapeDtypeStruct((wide, 9 * sizes.c_mid), BF16),
            jax.ShapeDtypeStruct((wide, 9 * sizes.c_in), BF16),
            jax.ShapeDtypeStruct((1, 2 * wide), F32),
        ),
        in_specs=[any_spec] * 4 + [vmem, vmem, smem],
        out_specs=(any_spec,) * 4 + (vmem,),
        scratch_shapes=[
            pltpu.VMEM((2, sizes.columns, narrow), BF16),
            pltpu.VMEM((sizes.columns, wide), BF16),
            pltpu.VMEM((3, tall, sizes.c_in), BF16),
            pltpu.VMEM((3, tall, sizes.c_mid), BF16),
            pltpu.VMEM((rows, wide), F32),
            pltpu.VMEM((rows, wide), F32),
            pltpu.VMEM((rows, sizes.c_in), BF16),
            pltpu.VMEM((rows, tall), BF16),
            pltpu.VMEM((rows, tall), BF16),
            pltpu.VMEM((rows, wide), BF16),
            pltpu.VMEM((rows, wide), BF16),
            pltpu.VMEM((rows, narrow), BF16),
            pltpu.VMEM((sizes.columns, narrow), F32),
            pltpu.VMEM((pitch, wide), F32),
            pltpu.VMEM((pitch, wide), F32),
            pltpu.VMEM((pitch, wide), F32),
            pltpu.VMEM((4, pitch, wide), F32),
            pltpu.VMEM((tall, WINDOW), F32),
            pltpu.VMEM((8, 2 * wide), F32),
            pltpu.VMEM((4, 8, 2 * wide), F32),
            pltpu.VMEM((blocks, tall // 2, LANES), F32),
            pltpu.VMEM((blocks, tall, LANES), BF16),
        ]
        + [pltpu.VMEM((blocks, tall >> (step + 1), LANES), BF16) for step in range(4)] * 2
        + [
            dma((2,)),
            dma((18,)),
            dma((18,)),
            dma((2,)),
            dma((MAP,)),
            dma((MAP,)),
            dma((MAP,)),
            dma((MAP,)),
            dma((MAP,)),
            dma((MAP,)),
            dma((4,)),
            dma((4,)),
            dma((2,)),
            dma((blocks, 3)),
        ]
        + [dma((blocks,))] * 16,
        compiler_params=pltpu.CompilerParams(collective_id=0, has_side_effects=True, vmem_limit_bytes=63 * MIB),
        cost_estimate=pl.CostEstimate(flops=45 * 10**9, bytes_accessed=3 * 10**7, transcendentals=2 * 10**6),
    )(frames, cot, weight3, weight4, bias3, bias4, counts)


def kernel_device(frames, clip_counts, conv3_weight, conv3_bias, conv4_weight, conv4_bias, cotangent):
    wide = conv3_weight.shape[0]
    sizes = Sizes(frames.shape[1], 2, conv3_weight.shape[1] // 9, conv4_weight.shape[1] // 9)
    conv4_out, frames_grad, grad4, grad3, biases = net(
        sizes,
        clip_counts.shape[0],
        frames.T,
        cotangent.T,
        conv3_weight,
        conv4_weight,
        conv3_bias,
        conv4_bias,
        clip_counts,
    )
    return (
        conv4_out.T,
        frames_grad.T,
        grad3.astype(F32),
        biases[0, wide:],
        grad4.astype(F32),
        biases[0, :wide],
    )


def solution(mesh):
    in_specs = (
        P("chan", "dp"),
        P("dp"),
        P("chan", None),
        P("chan"),
        P("chan", None),
        P("chan"),
        P("chan", "dp"),
    )
    out_specs = (
        P("chan", "dp"),
        P("chan", "dp"),
        P("chan", None),
        P("chan"),
        P("chan", None),
        P("chan"),
    )
    fits = mesh.shape["chan"] == 2 and mesh.shape["dp"] == 16
    per_device = kernel_device if fits else general_device
    return jax.shard_map(
        per_device, mesh=mesh, in_specs=in_specs, out_specs=out_specs, check_vma=False
    )
```

```python
import functools

import jax
import jax.numpy as jnp
from jax import lax
from jax.experimental import pallas as pl
from jax.experimental.pallas import tpu as pltpu
from jax.sharding import PartitionSpec as P

MAP = 13
AREA = MAP * MAP
LANES = 128
WINDOW = 256
BATCH = 8
MESH = pl.DeviceIdType.MESH
F32 = jnp.float32
BF16 = jnp.bfloat16
MIB = 2**20


def shift_cols(values, offset):
    if offset == 0:
        return values
    if offset > 0:
        return jnp.pad(values[:, offset:], ((0, 0), (0, offset)))
    return jnp.pad(values[:, :offset], ((0, 0), (-offset, 0)))


def tap_table(count):
    pixel = jnp.arange(count, dtype=jnp.int32) % AREA
    row_of = pixel // MAP
    col_of = pixel % MAP
    table = []
    for tap in range(9):
        tap_row = tap // 3
        tap_col = tap % 3
        src_row = row_of + tap_row - 1
        src_col = col_of + tap_col - 1
        valid = (src_row >= 0) & (src_row < MAP) & (src_col >= 0) & (src_col < MAP)
        table.append(((tap_row - 1) * MAP + tap_col - 1, valid[None, :]))
    return table


def conv_forward(field, kernel, table):
    result = None
    for tap in range(9):
        offset, valid = table[tap]
        term = jnp.dot(kernel[:, tap, :], field, preferred_element_type=F32)
        term = jnp.where(valid, shift_cols(term, offset), 0.0)
        result = term if result is None else result + term
    return result


def conv_backward(grad_field, kernel, table):
    result = None
    for tap in range(9):
        offset, valid = table[tap]
        masked = jnp.where(valid, grad_field, jnp.zeros((), grad_field.dtype))
        moved = shift_cols(masked, -offset)
        term = jnp.einsum("dc,dp->cp", kernel[:, tap, :], moved, preferred_element_type=F32)
        result = term if result is None else result + term
    return result


def kernel_grad(field, grad_field, table):
    taps_out = []
    for tap in range(9):
        offset, valid = table[tap]
        masked = jnp.where(valid, grad_field, jnp.zeros((), grad_field.dtype))
        moved = shift_cols(masked, -offset)
        taps_out.append(jnp.einsum("dp,cp->dc", moved, field, preferred_element_type=F32))
    return jnp.concatenate(taps_out, axis=1)


def silu_slope(value, sigma):
    return sigma * (1.0 + value * (1.0 - sigma))


def unpack(flat, shapes):
    pieces = []
    offset = 0
    for shape in shapes:
        length = 1
        for extent in shape:
            length = length * extent
        pieces.append(flat[offset : offset + length].reshape(shape))
        offset = offset + length
    return pieces


def general_device(frames, clip_counts, conv3_weight, conv3_bias, conv4_weight, conv4_bias, cotangent):
    columns = frames.shape[1]
    frame_count = columns // AREA
    videos_here = clip_counts.shape[0]
    per_video = frame_count // videos_here
    out_width = conv3_weight.shape[0]
    frame_ids = jnp.arange(frame_count, dtype=jnp.int32)
    owner = (frame_ids // per_video)[:, None] == jnp.arange(videos_here, dtype=jnp.int32)[None, :]
    count_of = jnp.sum(jnp.where(owner, clip_counts[None, :], 0), axis=1)
    frame_alive = (frame_ids % per_video < count_of).astype(F32)
    alive = jnp.broadcast_to(frame_alive[:, None], (frame_count, AREA)).reshape(1, columns)
    table = tap_table(columns)
    kernel3 = conv3_weight.reshape(out_width, 9, -1)
    kernel4 = conv4_weight.reshape(out_width, 9, -1)
    full_input = lax.all_gather(frames, "chan", axis=0, tiled=True)
    pre3 = conv_forward(full_input, kernel3, table) + conv3_bias.astype(F32)[:, None]
    sigma3 = jax.nn.sigmoid(pre3)
    mid = (pre3 * sigma3).astype(BF16)
    full_mid = lax.all_gather(mid, "chan", axis=0, tiled=True)
    pre4 = conv_forward(full_mid, kernel4, table) + conv4_bias.astype(F32)[:, None]
    sigma4 = jax.nn.sigmoid(pre4)
    conv4_out = (alive * pre4 * sigma4).astype(BF16)
    grad4 = (cotangent.astype(F32) * alive * silu_slope(pre4, sigma4)).astype(BF16)
    kernel4_local = kernel_grad(full_mid, grad4, table)
    bias4_local = jnp.sum(grad4.astype(F32), axis=1)
    shapes4 = (kernel4_local.shape, bias4_local.shape)
    partial_terms = conv_backward(grad4, kernel4, table)
    grad_mid = lax.psum_scatter(partial_terms, "chan", scatter_dimension=0, tiled=True)
    grad3 = (grad_mid * silu_slope(pre3, sigma3)).astype(BF16)
    kernel3_local = kernel_grad(full_input, grad3, table)
    bias3_local = jnp.sum(grad3.astype(F32), axis=1)
    shapes3 = (kernel3_local.shape, bias3_local.shape)
    input_terms = conv_backward(grad3, kernel3, table)
    frames_grad = lax.psum_scatter(input_terms, "chan", scatter_dimension=0, tiled=True)
    packed = jnp.concatenate(
        [item.reshape(-1) for item in (kernel3_local, bias3_local, kernel4_local, bias4_local)]
    )
    whole = lax.psum(packed, "dp")
    conv3_weight_grad, conv3_bias_grad, conv4_weight_grad, conv4_bias_grad = unpack(
        whole, shapes3 + shapes4
    )
    return (
        conv4_out,
        frames_grad,
        conv3_weight_grad,
        conv3_bias_grad,
        conv4_weight_grad,
        conv4_bias_grad,
    )


def up(value, unit):
    return -(-value // unit) * unit


def aligned(value, unit):
    return pl.multiple_of(value, unit)


class Sizes:
    def __init__(self, columns, chan, c_in, c_mid):
        self.columns = columns
        self.frames = columns // AREA
        self.used = self.frames * MAP
        self.pitch = up(self.used, 16)
        self.rows = MAP * self.pitch
        self.c_in, self.c_mid = c_in, c_mid
        self.own_in, self.own_mid = c_in // chan, c_mid // chan
        self.tall = 3 * self.own_mid
        self.blocks4, self.blocks3 = 3 * c_mid // LANES, 3 * c_in // LANES
        self.blocks = self.blocks4 + self.blocks3

    def slab(self, y):
        return slice(y * self.pitch, (y + 1) * self.pitch)

    def slabs(self, first, end):
        return pl.ds(first * self.pitch, (end - first) * self.pitch)


def column_masks(sizes, width):
    row = lax.broadcasted_iota(jnp.int32, (sizes.pitch, width), 0).astype(F32)
    frame = jnp.floor((row + 0.5) * (1.0 / MAP))
    col = row - frame * MAP
    used = row < sizes.used
    return frame, used, used & (col > 0.5), used & (col < MAP - 1.5)


def loop(count, body):
    def step(index, carry):
        body(index)
        return carry

    lax.fori_loop(0, count, step, 0)


def frame_batches(sizes, flat, slabs, move):
    whole = sizes.frames // BATCH

    def body(index):
        part = flat.at[pl.ds(aligned(index * (BATCH * AREA), 8), BATCH * AREA)]
        at = index * (BATCH * MAP)
        rows = [slabs.at[pl.ds(aligned(y * sizes.pitch + at, 8), BATCH * MAP)] for y in range(MAP)]
        for f in range(BATCH):
            for y in range(MAP):
                move(part, f * AREA + y * MAP, rows[y], f * MAP)

    if whole:
        loop(whole, body)
    for f in range(whole * BATCH, sizes.frames):
        for y in range(MAP):
            move(flat, f * AREA + y * MAP, slabs, y * sizes.pitch + f * MAP)


def to_slabs(sizes, flat, slabs, lanes):
    def move(source, source_at, target, target_at):
        target[target_at : target_at + MAP, lanes] = source[source_at : source_at + MAP, lanes]

    frame_batches(sizes, flat, slabs, move)


def from_slabs(sizes, slabs, flat, lanes):
    def move(target, target_at, source, source_at):
        target[target_at : target_at + MAP, :] = source[source_at : source_at + MAP, lanes]

    frame_batches(sizes, flat, slabs, move)


def windows(sizes, move):
    whole = sizes.columns // WINDOW
    loop(whole, lambda index: move(pl.ds(aligned(index * WINDOW, WINDOW), WINDOW)))
    if sizes.columns % WINDOW:
        move(slice(whole * WINDOW, sizes.columns))


def remote(source, target, send, recv, device):
    return pltpu.make_async_remote_copy(
        src_ref=source, dst_ref=target, send_sem=send, recv_sem=recv, device_id=device, device_id_type=MESH
    )


def weight_copies(me, weight, kept, sems, half):
    outputs = weight.shape[0]
    copies = []
    for tap in range(9):
        for part in range(2):
            source = aligned(tap * 2 * half + lax.rem(me + part, 2) * half, LANES)
            copies.append(
                pltpu.make_async_copy(
                    weight.at[:, pl.ds(source, half)],
                    kept.at[tap // 3, pl.ds((tap % 3) * outputs, outputs), pl.ds(part * half, half)],
                    sems.at[tap * 2 + part],
                )
            )
    return copies


def conv_terms(sizes, field, kept, y, depth):
    rows = [r for r in range(3) if 0 <= y + r - 1 < MAP]
    taps = jnp.concatenate([field[sizes.slab(y + r - 1), 0:depth] for r in rows], axis=1)
    width = kept.shape[1] // 3
    out = []
    for s in range(3):
        weights = jnp.concatenate([kept[r, s * width : (s + 1) * width, :] for r in rows], axis=1)
        out.append(lax.dot_general(taps, weights, (((1,), (1,)), ((), ())), preferred_element_type=F32))
    return out


def input_gradient(sizes, grads, kept, y):
    rows = [r for r in range(3) if 0 <= y + 1 - r < MAP]
    taps = jnp.concatenate([grads[sizes.slab(y + 1 - r), :] for r in rows], axis=1)
    weights = jnp.concatenate([kept[r] for r in rows], axis=0)
    return jnp.dot(taps, weights, preferred_element_type=F32)


def kernel_gradient(sizes, grads, values, r, lanes):
    span = sizes.rows - (sizes.pitch if r != 1 else 0)
    at = sizes.pitch if r == 0 else 0
    to = sizes.pitch if r == 2 else 0
    return lax.dot_general(
        grads[at : at + span, :], values[to : to + span, lanes], (((0,), (0,)), ((), ())), preferred_element_type=F32
    )


def before(value):
    return pltpu.roll(value, 1, 0)


def after(value):
    return pltpu.roll(value, value.shape[0] - 1, 0)


def sigmoid(value):
    return 1.0 / (1.0 + jnp.exp(-value))


def fold(value):
    return jnp.sum(value.reshape(value.shape[0] // 8, 8, value.shape[1]), axis=0)


class Ring:
    def __init__(self):
        self.dp = lax.axis_index("dp")
        self.me = lax.axis_index("chan")
        self.bits = [lax.rem(lax.div(self.dp, 2**bit), 2) for bit in range(4)]
        self.core = (self.dp, 1 - self.me)

    def across(self, bit):
        return (self.dp + 2**bit * (1 - 2 * self.bits[bit]), self.me)

    def side(self, step, kind):
        x, y = self.bits[:2]
        return x + kind * (y - x) if step == 0 else y + kind * (x - y)

    def partner(self, step, kind):
        apart = 1 + kind if step == 0 else 2 - kind
        return (self.dp + apart * (1 - 2 * self.side(step, kind)), self.me)

    def along_z(self, mask):
        _, _, low, high = self.bits
        low = 1 - low if mask & 1 else low
        high = 1 - high if mask & 2 else high
        z = 2 * high + low
        return z, (z * 4 + lax.rem(self.dp, 4), self.me)


class GradientSum:
    def __init__(self, ring, keep, outs, ins, done, sems):
        self.ring, self.keep, self.outs, self.ins, self.done = ring, keep, outs, ins, done
        self.sends, self.recvs = sems[:6], sems[6:]
        self.size = done.shape[1]

    def kept_quarter(self, kind, mine):
        side = self.ring.side(1, kind)
        return (side if mine else 1 - side) * (self.size // 4)

    def kept_piece(self, kind, z):
        return pl.ds(aligned(self.kept_quarter(kind, True) + z * (self.size // 16), 16), self.size // 16)

    def finished(self, step, kind):
        at = self.ring.side(0, kind) * (self.size // 2)
        if step > 0:
            at = at + self.ring.side(1, kind) * (self.size // 4)
        if step > 1:
            at = at + self.ring.along_z(0)[0] * (self.size // 16)
        return pl.ds(aligned(at, 16), self.size // (2, 4, 16)[step])

    def down(self, step, j, kind):
        if step < 2:
            return [
                remote(
                    self.outs[step].at[j],
                    self.ins[step].at[j],
                    self.sends[step].at[j],
                    self.recvs[step].at[j],
                    self.ring.partner(step, kind),
                )
            ]
        return [
            remote(
                self.outs[2].at[j, mask - 1],
                self.ins[2].at[j, mask - 1],
                self.sends[2].at[j, mask - 1],
                self.recvs[2].at[j, mask - 1],
                self.ring.along_z(mask)[1],
            )
            for mask in (1, 2, 3)
        ]

    def back(self, step, j, kind):
        rows = self.done.at[j, self.finished(step, kind)]
        sends, recvs = self.sends[5 - step], self.recvs[5 - step]
        if step < 2:
            return [remote(rows, rows, sends.at[j], recvs.at[j], self.ring.partner(step, kind))]
        return [
            remote(rows, rows, sends.at[j, mask - 1], recvs.at[j, mask - 1], self.ring.along_z(mask)[1])
            for mask in (1, 2, 3)
        ]

    def stage(self, number, j, kind):
        quarter = self.size // 4
        if number:
            for copy in self.down(number - 1, j, kind) if number < 4 else self.back(6 - number, j, kind):
                copy.wait()
        if number == 1:
            mine = pl.ds(aligned(self.kept_quarter(kind, True), 16), quarter)
            sent = pl.ds(aligned(self.kept_quarter(kind, False), 16), quarter)
            self.keep[j, mine, :] = self.keep[j, mine, :] + self.ins[0][j, mine, :].astype(F32)
            self.outs[1][j] = (self.keep[j, sent, :] + self.ins[0][j, sent, :].astype(F32)).astype(BF16)
        elif number == 2:
            mine = pl.ds(aligned(self.kept_quarter(kind, True), 16), quarter)
            self.keep[j, mine, :] = self.keep[j, mine, :] + self.ins[1][j].astype(F32)
            for mask in (1, 2, 3):
                self.outs[2][j, mask - 1] = self.keep[j, self.kept_piece(kind, self.ring.along_z(mask)[0]), :].astype(BF16)
        elif number == 3:
            total = self.keep[j, self.kept_piece(kind, self.ring.along_z(0)[0]), :]
            for mask in (1, 2, 3):
                total = total + self.ins[2][j, mask - 1].astype(F32)
            self.done[j, self.finished(2, kind), :] = total.astype(BF16)
        if number < 6:
            for copy in self.down(number, j, kind) if number < 3 else self.back(5 - number, j, kind):
                copy.start()

    def run(self, number, first, count):
        def body(index):
            j = first + index
            self.stage(number, j, lax.rem(j, 2))

        loop(count, body)


def net_kernel(
    sizes,
    videos,
    frames_hbm,
    cot_hbm,
    weight3_hbm,
    weight4_hbm,
    bias3,
    bias4,
    counts,
    conv_hbm,
    frames_grad_hbm,
    grad4_hbm,
    grad3_hbm,
    bias_grads,
    frames,
    cot,
    kept3,
    kept4,
    flat,
    slabs,
    field,
    mid,
    shifted4,
    outgoing,
    incoming,
    last_in,
    frames_field,
    left,
    right,
    alive,
    stash,
    result,
    bias_sum,
    bias_in,
    keep,
    done,
    out0,
    out1,
    out2,
    in0,
    in1,
    in2,
    load_sems,
    kept3_sems,
    kept4_sems,
    frame_sems,
    mid_send,
    mid_recv,
    out_send,
    out_recv,
    last_send,
    last_recv,
    bias_send,
    bias_recv,
    store_sems,
    block_sems,
    *sum_sems,
):
    ring = Ring()
    me = ring.me
    pitch, wide, narrow = sizes.pitch, sizes.own_mid, sizes.own_in
    slab = sizes.slab
    shifted3 = mid

    own_load = pltpu.make_async_copy(frames_hbm, frames.at[0], load_sems.at[0])
    cot_load = pltpu.make_async_copy(cot_hbm, cot, load_sems.at[1])
    kept3_loads = weight_copies(me, weight3_hbm, kept3, kept3_sems, narrow)
    kept4_loads = weight_copies(me, weight4_hbm, kept4, kept4_sems, wide)
    own_load.start()
    barrier = pltpu.get_barrier_semaphore()
    partners = [ring.core, ring.across(0), ring.across(1)] + [ring.along_z(mask)[1] for mask in (1, 2, 3)]
    for partner in partners:
        pl.semaphore_signal(barrier, inc=1, device_id=partner, device_id_type=MESH)
    for copy in [cot_load] + kept3_loads + kept4_loads:
        copy.start()
    for y in range(MAP):
        slabs[(y + 1) * pitch - 16 : (y + 1) * pitch, :] = jnp.zeros((16, wide), F32)

    def bring(source, lanes, target):
        def widen(rows):
            flat[rows, lanes] = source[rows, :].astype(F32)

        windows(sizes, widen)
        to_slabs(sizes, flat, slabs, lanes)

        def pack(y):
            rows = pl.ds(aligned(y * pitch, 16), pitch)
            target[rows, lanes] = slabs[rows, lanes].astype(BF16)

        loop(MAP, pack)

    own_load.wait()
    bring(frames.at[0], slice(0, narrow), field)
    pl.semaphore_wait(barrier, len(partners))
    swap_frames = remote(frames_hbm, frames.at[1], frame_sems.at[0], frame_sems.at[1], ring.core)
    swap_frames.start()
    frame, used, has_left, has_right = column_masks(sizes, wide)
    per_video = sizes.frames // videos
    live = None
    for v in range(videos):
        low = v * per_video - 0.5
        here = (frame > low) & (frame < low + per_video) & (frame < low + counts[v].astype(F32))
        live = here if live is None else live | here
    left[...] = has_left.astype(F32)
    right[...] = has_right.astype(F32)
    alive[...] = (live & used).astype(F32)
    bias_sum[...] = jnp.zeros(bias_sum.shape, F32)
    cot_load.wait()
    bring(cot, slice(0, wide), outgoing)
    swap_frames.wait()
    bring(frames.at[1], slice(narrow, 2 * narrow), field)
    for copy in kept3_loads:
        copy.wait()

    def swap_mid(number):
        rows = sizes.slabs(*THIRDS[number])
        return remote(
            mid.at[rows, 0:wide], mid.at[rows, wide : 2 * wide], mid_send.at[number], mid_recv.at[number], ring.core
        )

    def joined(terms, bias):
        minus, centre, plus = terms
        return centre + before(minus) * left[...] + after(plus) * right[...] + bias[...].astype(F32).reshape(1, -1)

    def finish3(y, terms):
        value = joined(terms, bias3)
        sigma = sigmoid(value)
        mid[slab(y), 0:wide] = (value * sigma).astype(BF16)
        flat[slab(y), :] = silu_slope(value, sigma)
        for number, (_, end) in enumerate(THIRDS):
            if y == end - 1:
                swap_mid(number).start()

    waiting = None
    for y in range(MAP):
        terms = conv_terms(sizes, field, kept3, y, sizes.c_in)
        if waiting is not None:
            finish3(*waiting)
        waiting = (y, terms)
    finish3(*waiting)

    def shift_out(target, y, rounded):
        grad = rounded.astype(F32)
        target[slab(y), 0:wide] = (after(grad) * right[...]).astype(BF16)
        target[slab(y), wide : 2 * wide] = rounded
        target[slab(y), 2 * wide : 3 * wide] = (before(grad) * left[...]).astype(BF16)
        return fold(grad)

    def finish4(y, terms):
        value = joined(terms, bias4)
        sigma = sigmoid(value)
        on = alive[...]
        slabs[slab(y), :] = on * value * sigma
        return shift_out(
            shifted4, y, (outgoing[slab(y), :].astype(F32) * on * silu_slope(value, sigma)).astype(BF16)
        )

    for copy in kept4_loads:
        copy.wait()
    summed = jnp.zeros((8, wide), F32)
    waiting = None
    for y in range(MAP):
        if y == 0:
            swap_mid(0).wait()
            swap_mid(1).wait()
        if y == THIRDS[1][1] - 1:
            swap_mid(2).wait()
            swap_mid(3).wait()
        terms = conv_terms(sizes, mid, kept4, y, sizes.c_mid)
        if waiting is not None:
            summed = summed + finish4(*waiting)
        waiting = (y, terms)
    bias_sum[:, 0:wide] = summed + finish4(*waiting)

    total = GradientSum(ring, keep, (out0, out1, out2), (in0, in1, in2), done, sum_sems)
    run = total.run
    half = sizes.tall // 2

    def give(value, number):
        result[...] = value
        for part in range(2):
            side = ring.side(0, (number + part) % 2)
            lanes = slice(part * LANES, (part + 1) * LANES)
            keep[number + part] = result[pl.ds(aligned(side * half, 16), half), lanes]
            out0[number + part] = result[pl.ds(aligned((1 - side) * half, 16), half), lanes].astype(BF16)
            total.stage(0, number + part, (number + part) % 2)

    step = 0
    events = EVENTS["kernel4"]
    for r in range(3):
        for part in range(sizes.c_mid // WINDOW):
            lanes = slice(part * WINDOW, (part + 1) * WINDOW)
            give(kernel_gradient(sizes, shifted4, mid, r, lanes), 2 * step)
            for event in events.get(step, ()):
                run(*event)
            step += 1

    def swap4(number):
        rows = sizes.slabs(*PAIRS[number])
        return remote(outgoing.at[rows], incoming.at[rows], out_send.at[number], out_recv.at[number], ring.core)

    def finish_back(y):
        value = stash[y % 6] + incoming[slab(y), :].astype(F32)
        return shift_out(shifted3, y, (value * flat[slab(y), :]).astype(BF16))

    summed = jnp.zeros((8, wide), F32)
    events = EVENTS["input4"]
    for number in range(len(PAIRS) + 2):
        if number >= 2:
            swap4(number - 2).wait()
        late = list(range(*PAIRS[number - 2])) if number >= 2 else []
        for y in range(*PAIRS[number]) if number < len(PAIRS) else ():
            grad = input_gradient(sizes, shifted4, kept4, y)
            stash[y % 6] = grad[:, 0:wide]
            outgoing[slab(y), :] = grad[:, wide : 2 * wide].astype(BF16)
            if late:
                summed = summed + finish_back(late.pop(0))
        for y in late:
            summed = summed + finish_back(y)
        if number < len(PAIRS):
            swap4(number).start()
        for event in events.get(number, ()):
            run(*event)
    bias_sum[:, wide : 2 * wide] = summed

    def swap_bias(bit):
        return remote(bias_sum, bias_in.at[bit], bias_send.at[bit], bias_recv.at[bit], ring.across(bit))

    def add_bias(bit):
        swap_bias(bit).wait()
        bias_sum[...] = bias_sum[...] + bias_in[bit]

    swap_bias(0).start()
    events = EVENTS["kernel3"]
    for r in range(3):
        give(kernel_gradient(sizes, shifted3, field, r, slice(0, sizes.c_in)), 2 * step)
        for event in events.get(r, ()):
            run(*event)
        if r != 1:
            add_bias(r // 2)
            swap_bias(r // 2 + 1).start()
        step += 1

    from_slabs(sizes, slabs, flat, slice(0, wide))

    def narrow_down(rows):
        cot[rows, :] = flat[rows, :].astype(BF16)

    windows(sizes, narrow_down)
    conv_store = pltpu.make_async_copy(cot, conv_hbm, store_sems.at[0])
    conv_store.start()
    add_bias(2)
    swap_bias(3).start()
    for event in EVENTS["between"]:
        run(*event)

    def swap3(number):
        rows = sizes.slabs(*THIRDS[number])
        return remote(
            outgoing.at[rows, 0:narrow], last_in.at[rows], last_send.at[number], last_recv.at[number], ring.core
        )

    events = EVENTS["input3"]
    for y in range(MAP):
        grad = input_gradient(sizes, shifted3, kept3, y)
        slabs[slab(y), 0:narrow] = grad[:, 0:narrow]
        outgoing[slab(y), 0:narrow] = grad[:, narrow : 2 * narrow].astype(BF16)
        for number, (_, end) in enumerate(THIRDS):
            if y == end - 1:
                swap3(number).start()
        for event in events.get(y, ()):
            run(*event)
    add_bias(3)
    for number in range(len(THIRDS)):
        swap3(number).wait()

    def join(y):
        rows = pl.ds(aligned(y * pitch, 16), pitch)
        slabs[rows, 0:narrow] = slabs[rows, 0:narrow] + last_in[rows, :].astype(F32)

    loop(MAP, join)
    from_slabs(sizes, slabs, frames_field, slice(0, narrow))
    frames_store = pltpu.make_async_copy(frames_field, frames_grad_hbm, store_sems.at[1])
    frames_store.start()

    def block_stores(j, grad_hbm, first, parts):
        r, part = lax.div(j - first, parts), lax.rem(j - first, parts)
        column_block = lax.rem(part + me * (parts // 2), parts)
        out = []
        for s in range(3):
            at = aligned(((r * 3 + s) * parts + column_block) * LANES, LANES)
            out.append(
                pltpu.make_async_copy(
                    done.at[j, pl.ds(s * wide, wide)], grad_hbm.at[:, pl.ds(at, LANES)], block_sems.at[j, s]
                )
            )
        return out

    def stores4(j):
        return block_stores(j, grad4_hbm, 0, sizes.c_mid // LANES)

    def stores3(j):
        return block_stores(j, grad3_hbm, sizes.blocks4, sizes.c_in // LANES)

    def save(stores, first, count):
        def body(index):
            j = first + index
            total.stage(6, j, lax.rem(j, 2))
            for copy in stores(j):
                copy.start()

        loop(count, body)

    def saved(stores, first, count):
        def body(index):
            for copy in stores(first + index):
                copy.wait()

        loop(count, body)

    for event in EVENTS["last"]:
        if event[0] == 6:
            save(stores4 if event[1] < sizes.blocks4 else stores3, event[1], event[2])
        else:
            run(*event)
    bias_grads[...] = jnp.sum(bias_sum[...], axis=0, keepdims=True)
    conv_store.wait()
    frames_store.wait()
    saved(stores4, 0, sizes.blocks4)
    saved(stores3, sizes.blocks4, sizes.blocks3)


THIRDS = ((0, 4), (4, 7), (7, 10), (10, 13))
PAIRS = tuple((y, min(y + 2, MAP)) for y in range(0, MAP, 2))
EVENTS = {
    "kernel4": {
        3: [(1, 0, 2)],
        4: [(1, 2, 2)],
        5: [(1, 4, 2)],
    },
    "input4": {
        0: [(1, 6, 2)],
        1: [(2, 0, 2)],
        2: [(1, 8, 2), (2, 2, 2)],
        3: [(1, 10, 2), (2, 4, 2)],
        4: [(3, 0, 2), (2, 6, 2), (2, 8, 2)],
        5: [(3, 2, 2), (2, 10, 2)],
        6: [(3, 4, 2)],
        8: [(4, 0, 2)],
    },
    "kernel3": {
        0: [(3, 6, 2)],
        1: [(3, 8, 2), (5, 0, 2)],
        2: [(4, 2, 2), (1, 12, 2), (3, 10, 2)],
    },
    "between": [(4, 4, 2), (1, 14, 2)],
    "input3": {
        3: [(4, 6, 2)],
        7: [(4, 8, 2), (1, 16, 2)],
        9: [(5, 2, 2)],
        11: [(4, 10, 2), (2, 12, 2)],
    },
    "last": [
        (6, 0, 2), (5, 4, 2), (2, 14, 2), (5, 6, 2), (5, 8, 2), (2, 16, 2), (3, 12, 2), (6, 2, 2),
        (5, 10, 2), (3, 14, 2), (6, 4, 2), (3, 16, 2), (6, 6, 2), (4, 12, 2), (6, 8, 2), (4, 14, 2),
        (6, 10, 2), (4, 16, 2), (5, 12, 2), (5, 14, 2), (5, 16, 2), (6, 12, 2), (6, 14, 2), (6, 16, 2),
    ],
}


def net(sizes, videos, frames, cot, weight3, weight4, bias3, bias4, counts):
    any_spec = pl.BlockSpec(memory_space=pl.ANY)
    vmem = pl.BlockSpec(memory_space=pltpu.VMEM)
    smem = pl.BlockSpec(memory_space=pltpu.SMEM)
    wide, narrow, pitch, rows, tall = sizes.own_mid, sizes.own_in, sizes.pitch, sizes.rows, sizes.tall
    blocks = sizes.blocks
    dma = pltpu.SemaphoreType.DMA
    return pl.pallas_call(
        functools.partial(net_kernel, sizes, videos),
        out_shape=(
            jax.ShapeDtypeStruct((sizes.columns, wide), BF16),
            jax.ShapeDtypeStruct((sizes.columns, narrow), F32),
            jax.ShapeDtypeStruct((wide, 9 * sizes.c_mid), BF16),
            jax.ShapeDtypeStruct((wide, 9 * sizes.c_in), BF16),
            jax.ShapeDtypeStruct((1, 2 * wide), F32),
        ),
        in_specs=[any_spec] * 4 + [vmem, vmem, smem],
        out_specs=(any_spec,) * 4 + (vmem,),
        scratch_shapes=[
            pltpu.VMEM((2, sizes.columns, narrow), BF16),
            pltpu.VMEM((sizes.columns, wide), BF16),
            pltpu.VMEM((3, tall, sizes.c_in), BF16),
            pltpu.VMEM((3, tall, sizes.c_mid), BF16),
            pltpu.VMEM((rows, wide), F32),
            pltpu.VMEM((rows, wide), F32),
            pltpu.VMEM((rows, sizes.c_in), BF16),
            pltpu.VMEM((rows, tall), BF16),
            pltpu.VMEM((rows, tall), BF16),
            pltpu.VMEM((rows, wide), BF16),
            pltpu.VMEM((rows, wide), BF16),
            pltpu.VMEM((rows, narrow), BF16),
            pltpu.VMEM((sizes.columns, narrow), F32),
            pltpu.VMEM((pitch, wide), F32),
            pltpu.VMEM((pitch, wide), F32),
            pltpu.VMEM((pitch, wide), F32),
            pltpu.VMEM((6, pitch, wide), F32),
            pltpu.VMEM((tall, WINDOW), F32),
            pltpu.VMEM((8, 2 * wide), F32),
            pltpu.VMEM((4, 8, 2 * wide), F32),
            pltpu.VMEM((blocks, tall // 2, LANES), F32),
            pltpu.VMEM((blocks, tall, LANES), BF16),
        ]
        + [
            pltpu.VMEM((blocks, tall // 2, LANES), BF16),
            pltpu.VMEM((blocks, tall // 4, LANES), BF16),
            pltpu.VMEM((blocks, 3, tall // 16, LANES), BF16),
        ]
        * 2
        + [
            dma((2,)),
            dma((18,)),
            dma((18,)),
            dma((2,)),
            dma((MAP,)),
            dma((MAP,)),
            dma((MAP,)),
            dma((MAP,)),
            dma((MAP,)),
            dma((MAP,)),
            dma((4,)),
            dma((4,)),
            dma((2,)),
            dma((blocks, 3)),
        ]
        + [dma((blocks,)), dma((blocks,)), dma((blocks, 3)), dma((blocks, 3)), dma((blocks,)), dma((blocks,))] * 2,
        compiler_params=pltpu.CompilerParams(collective_id=0, has_side_effects=True, vmem_limit_bytes=63 * MIB),
        cost_estimate=pl.CostEstimate(flops=45 * 10**9, bytes_accessed=3 * 10**7, transcendentals=2 * 10**6),
    )(frames, cot, weight3, weight4, bias3, bias4, counts)


def end_kernel(conv, frames_grad, grad3, grad4, biases, conv_out, frames_out, wide3, bias3, wide4, bias4, *scratch):
    narrow3, narrow4, full3, full4, conv_kept, frames_kept, load_sems, store_sems = scratch
    passed = []
    for number, (source, kept, target) in enumerate(((conv, conv_kept, conv_out), (frames_grad, frames_kept, frames_out))):
        passed.append(
            (
                pltpu.make_async_copy(source, kept, load_sems.at[6 + number]),
                pltpu.make_async_copy(kept, target, store_sems.at[6 + number]),
            )
        )
    parts = []
    for number, (source, small, large, target) in enumerate(
        ((grad4, narrow4, full4, wide4), (grad3, narrow3, full3, wide3))
    ):
        span = source.shape[1] // 3
        for part in range(3):
            lanes = pl.ds(part * span, span)
            at = 3 * number + part
            parts.append(
                (
                    pltpu.make_async_copy(source.at[:, lanes], small.at[:, lanes], load_sems.at[at]),
                    small,
                    large,
                    lanes,
                    pltpu.make_async_copy(large.at[:, lanes], target.at[:, lanes], store_sems.at[at]),
                )
            )
    for part in parts:
        part[0].start()
    for load, _ in passed:
        load.start()
    half = biases.shape[1] // 2
    bias4[...] = biases[0, 0:half]
    bias3[...] = biases[0, half:]
    for load, small, large, lanes, store in parts:
        load.wait()
        large[:, lanes] = small[:, lanes].astype(F32)
        store.start()
    for load, store in passed:
        load.wait()
        store.start()
    for part in parts:
        part[4].wait()
    for _, store in passed:
        store.wait()


def end(conv, frames_grad, grad3, grad4, biases):
    any_spec = pl.BlockSpec(memory_space=pl.ANY)
    vmem = pl.BlockSpec(memory_space=pltpu.VMEM)
    bias = jax.ShapeDtypeStruct((biases.shape[1] // 2,), F32)
    dma = pltpu.SemaphoreType.DMA
    return pl.pallas_call(
        end_kernel,
        out_shape=(
            jax.ShapeDtypeStruct(conv.shape, conv.dtype),
            jax.ShapeDtypeStruct(frames_grad.shape, F32),
            jax.ShapeDtypeStruct(grad3.shape, F32),
            bias,
            jax.ShapeDtypeStruct(grad4.shape, F32),
            bias,
        ),
        in_specs=[any_spec] * 4 + [vmem],
        out_specs=(any_spec, any_spec, any_spec, vmem, any_spec, vmem),
        scratch_shapes=[
            pltpu.VMEM(grad3.shape, BF16),
            pltpu.VMEM(grad4.shape, BF16),
            pltpu.VMEM(grad3.shape, F32),
            pltpu.VMEM(grad4.shape, F32),
            pltpu.VMEM(conv.shape, conv.dtype),
            pltpu.VMEM(frames_grad.shape, F32),
            dma((8,)),
            dma((8,)),
        ],
        compiler_params=pltpu.CompilerParams(vmem_limit_bytes=63 * MIB),
        cost_estimate=pl.CostEstimate(flops=10**7, bytes_accessed=2 * 10**7, transcendentals=0),
    )(conv, frames_grad, grad3, grad4, biases)


def kernel_device(frames, clip_counts, conv3_weight, conv3_bias, conv4_weight, conv4_bias, cotangent):
    sizes = Sizes(frames.shape[1], 2, conv3_weight.shape[1] // 9, conv4_weight.shape[1] // 9)
    results = net(
        sizes,
        clip_counts.shape[0],
        frames.T,
        cotangent.T,
        conv3_weight,
        conv4_weight,
        conv3_bias,
        conv4_bias,
        clip_counts,
    )
    conv4_out, frames_grad, grad3, bias3, grad4, bias4 = end(
        results[0], results[1], results[3], results[2], results[4]
    )
    return conv4_out.T, frames_grad.T, grad3, bias3, grad4, bias4


def solution(mesh):
    in_specs = (
        P("chan", "dp"),
        P("dp"),
        P("chan", None),
        P("chan"),
        P("chan", None),
        P("chan"),
        P("chan", "dp"),
    )
    out_specs = (
        P("chan", "dp"),
        P("chan", "dp"),
        P("chan", None),
        P("chan"),
        P("chan", None),
        P("chan"),
    )
    fits = mesh.shape["chan"] == 2 and mesh.shape["dp"] == 16
    per_device = kernel_device if fits else general_device
    return jax.shard_map(
        per_device, mesh=mesh, in_specs=in_specs, out_specs=out_specs, check_vma=False
    )
```

```python
import functools

import jax
import jax.numpy as jnp
from jax import lax
from jax.experimental import pallas as pl
from jax.experimental.pallas import tpu as pltpu
from jax.sharding import PartitionSpec as P

MAP = 13
AREA = MAP * MAP
LANES = 128
WINDOW = 256
BATCH = 8
MESH = pl.DeviceIdType.MESH
F32 = jnp.float32
BF16 = jnp.bfloat16
MIB = 2**20


def shift_cols(values, offset):
    if offset == 0:
        return values
    if offset > 0:
        return jnp.pad(values[:, offset:], ((0, 0), (0, offset)))
    return jnp.pad(values[:, :offset], ((0, 0), (-offset, 0)))


def tap_table(count):
    pixel = jnp.arange(count, dtype=jnp.int32) % AREA
    row_of = pixel // MAP
    col_of = pixel % MAP
    table = []
    for tap in range(9):
        tap_row = tap // 3
        tap_col = tap % 3
        src_row = row_of + tap_row - 1
        src_col = col_of + tap_col - 1
        valid = (src_row >= 0) & (src_row < MAP) & (src_col >= 0) & (src_col < MAP)
        table.append(((tap_row - 1) * MAP + tap_col - 1, valid[None, :]))
    return table


def conv_forward(field, kernel, table):
    result = None
    for tap in range(9):
        offset, valid = table[tap]
        term = jnp.dot(kernel[:, tap, :], field, preferred_element_type=F32)
        term = jnp.where(valid, shift_cols(term, offset), 0.0)
        result = term if result is None else result + term
    return result


def conv_backward(grad_field, kernel, table):
    result = None
    for tap in range(9):
        offset, valid = table[tap]
        masked = jnp.where(valid, grad_field, jnp.zeros((), grad_field.dtype))
        moved = shift_cols(masked, -offset)
        term = jnp.einsum("dc,dp->cp", kernel[:, tap, :], moved, preferred_element_type=F32)
        result = term if result is None else result + term
    return result


def kernel_grad(field, grad_field, table):
    taps_out = []
    for tap in range(9):
        offset, valid = table[tap]
        masked = jnp.where(valid, grad_field, jnp.zeros((), grad_field.dtype))
        moved = shift_cols(masked, -offset)
        taps_out.append(jnp.einsum("dp,cp->dc", moved, field, preferred_element_type=F32))
    return jnp.concatenate(taps_out, axis=1)


def silu_slope(value, sigma):
    return sigma * (1.0 + value * (1.0 - sigma))


def unpack(flat, shapes):
    pieces = []
    offset = 0
    for shape in shapes:
        length = 1
        for extent in shape:
            length = length * extent
        pieces.append(flat[offset : offset + length].reshape(shape))
        offset = offset + length
    return pieces


def general_device(frames, clip_counts, conv3_weight, conv3_bias, conv4_weight, conv4_bias, cotangent):
    columns = frames.shape[1]
    frame_count = columns // AREA
    videos_here = clip_counts.shape[0]
    per_video = frame_count // videos_here
    out_width = conv3_weight.shape[0]
    frame_ids = jnp.arange(frame_count, dtype=jnp.int32)
    owner = (frame_ids // per_video)[:, None] == jnp.arange(videos_here, dtype=jnp.int32)[None, :]
    count_of = jnp.sum(jnp.where(owner, clip_counts[None, :], 0), axis=1)
    frame_alive = (frame_ids % per_video < count_of).astype(F32)
    alive = jnp.broadcast_to(frame_alive[:, None], (frame_count, AREA)).reshape(1, columns)
    table = tap_table(columns)
    kernel3 = conv3_weight.reshape(out_width, 9, -1)
    kernel4 = conv4_weight.reshape(out_width, 9, -1)
    full_input = lax.all_gather(frames, "chan", axis=0, tiled=True)
    pre3 = conv_forward(full_input, kernel3, table) + conv3_bias.astype(F32)[:, None]
    sigma3 = jax.nn.sigmoid(pre3)
    mid = (pre3 * sigma3).astype(BF16)
    full_mid = lax.all_gather(mid, "chan", axis=0, tiled=True)
    pre4 = conv_forward(full_mid, kernel4, table) + conv4_bias.astype(F32)[:, None]
    sigma4 = jax.nn.sigmoid(pre4)
    conv4_out = (alive * pre4 * sigma4).astype(BF16)
    grad4 = (cotangent.astype(F32) * alive * silu_slope(pre4, sigma4)).astype(BF16)
    kernel4_local = kernel_grad(full_mid, grad4, table)
    bias4_local = jnp.sum(grad4.astype(F32), axis=1)
    shapes4 = (kernel4_local.shape, bias4_local.shape)
    partial_terms = conv_backward(grad4, kernel4, table)
    grad_mid = lax.psum_scatter(partial_terms, "chan", scatter_dimension=0, tiled=True)
    grad3 = (grad_mid * silu_slope(pre3, sigma3)).astype(BF16)
    kernel3_local = kernel_grad(full_input, grad3, table)
    bias3_local = jnp.sum(grad3.astype(F32), axis=1)
    shapes3 = (kernel3_local.shape, bias3_local.shape)
    input_terms = conv_backward(grad3, kernel3, table)
    frames_grad = lax.psum_scatter(input_terms, "chan", scatter_dimension=0, tiled=True)
    packed = jnp.concatenate(
        [item.reshape(-1) for item in (kernel3_local, bias3_local, kernel4_local, bias4_local)]
    )
    whole = lax.psum(packed, "dp")
    conv3_weight_grad, conv3_bias_grad, conv4_weight_grad, conv4_bias_grad = unpack(
        whole, shapes3 + shapes4
    )
    return (
        conv4_out,
        frames_grad,
        conv3_weight_grad,
        conv3_bias_grad,
        conv4_weight_grad,
        conv4_bias_grad,
    )


def up(value, unit):
    return -(-value // unit) * unit


def aligned(value, unit):
    return pl.multiple_of(value, unit)


class Sizes:
    def __init__(self, columns, chan, c_in, c_mid):
        self.columns = columns
        self.frames = columns // AREA
        self.used = self.frames * MAP
        self.pitch = up(self.used, 16)
        self.rows = MAP * self.pitch
        self.c_in, self.c_mid = c_in, c_mid
        self.own_in, self.own_mid = c_in // chan, c_mid // chan
        self.tall = 3 * self.own_mid
        self.blocks4, self.blocks3 = 3 * c_mid // LANES, 3 * c_in // LANES
        self.blocks = self.blocks4 + self.blocks3

    def slab(self, y):
        return slice(y * self.pitch, (y + 1) * self.pitch)

    def slabs(self, first, end):
        return pl.ds(first * self.pitch, (end - first) * self.pitch)


def column_masks(sizes, width):
    row = lax.broadcasted_iota(jnp.int32, (sizes.pitch, width), 0).astype(F32)
    frame = jnp.floor((row + 0.5) * (1.0 / MAP))
    col = row - frame * MAP
    used = row < sizes.used
    return frame, used, used & (col > 0.5), used & (col < MAP - 1.5)


def loop(count, body):
    def step(index, carry):
        body(index)
        return carry

    lax.fori_loop(0, count, step, 0)


def frame_batches(sizes, flat, slabs, move):
    whole = sizes.frames // BATCH

    def body(index):
        part = flat.at[pl.ds(aligned(index * (BATCH * AREA), 8), BATCH * AREA)]
        at = index * (BATCH * MAP)
        rows = [slabs.at[pl.ds(aligned(y * sizes.pitch + at, 8), BATCH * MAP)] for y in range(MAP)]
        for f in range(BATCH):
            for y in range(MAP):
                move(part, f * AREA + y * MAP, rows[y], f * MAP)

    if whole:
        loop(whole, body)
    for f in range(whole * BATCH, sizes.frames):
        for y in range(MAP):
            move(flat, f * AREA + y * MAP, slabs, y * sizes.pitch + f * MAP)


def to_slabs(sizes, flat, slabs, lanes):
    def move(source, source_at, target, target_at):
        target[target_at : target_at + MAP, lanes] = source[source_at : source_at + MAP, lanes]

    frame_batches(sizes, flat, slabs, move)


def from_slabs(sizes, slabs, flat, lanes):
    def move(target, target_at, source, source_at):
        target[target_at : target_at + MAP, :] = source[source_at : source_at + MAP, lanes]

    frame_batches(sizes, flat, slabs, move)


def windows(sizes, move):
    whole = sizes.columns // WINDOW
    loop(whole, lambda index: move(pl.ds(aligned(index * WINDOW, WINDOW), WINDOW)))
    if sizes.columns % WINDOW:
        move(slice(whole * WINDOW, sizes.columns))


def remote(source, target, send, recv, device):
    return pltpu.make_async_remote_copy(
        src_ref=source, dst_ref=target, send_sem=send, recv_sem=recv, device_id=device, device_id_type=MESH
    )


def weight_copies(me, weight, kept, sems, half):
    outputs = weight.shape[0]
    copies = []
    for tap in range(9):
        for part in range(2):
            source = aligned(tap * 2 * half + lax.rem(me + part, 2) * half, LANES)
            copies.append(
                pltpu.make_async_copy(
                    weight.at[:, pl.ds(source, half)],
                    kept.at[tap // 3, pl.ds((tap % 3) * outputs, outputs), pl.ds(part * half, half)],
                    sems.at[tap * 2 + part],
                )
            )
    return copies


def conv_terms(sizes, field, kept, y, depth):
    rows = [r for r in range(3) if 0 <= y + r - 1 < MAP]
    taps = jnp.concatenate([field[sizes.slab(y + r - 1), 0:depth] for r in rows], axis=1)
    width = kept.shape[1] // 3
    out = []
    for s in range(3):
        weights = jnp.concatenate([kept[r, s * width : (s + 1) * width, :] for r in rows], axis=1)
        out.append(lax.dot_general(taps, weights, (((1,), (1,)), ((), ())), preferred_element_type=F32))
    return out


def input_gradient(sizes, grads, kept, y):
    rows = [r for r in range(3) if 0 <= y + 1 - r < MAP]
    taps = jnp.concatenate([grads[sizes.slab(y + 1 - r), :] for r in rows], axis=1)
    weights = jnp.concatenate([kept[r] for r in rows], axis=0)
    return jnp.dot(taps, weights, preferred_element_type=F32)


def kernel_gradient(sizes, grads, values, r, lanes):
    span = sizes.rows - (sizes.pitch if r != 1 else 0)
    at = sizes.pitch if r == 0 else 0
    to = sizes.pitch if r == 2 else 0
    return lax.dot_general(
        grads[at : at + span, :], values[to : to + span, lanes], (((0,), (0,)), ((), ())), preferred_element_type=F32
    )


def before(value):
    return pltpu.roll(value, 1, 0)


def after(value):
    return pltpu.roll(value, value.shape[0] - 1, 0)


def sigmoid(value):
    return 1.0 / (1.0 + jnp.exp(-value))


def fold(value):
    return jnp.sum(value.reshape(value.shape[0] // 8, 8, value.shape[1]), axis=0)


class Ring:
    def __init__(self):
        self.dp = lax.axis_index("dp")
        self.me = lax.axis_index("chan")
        self.bits = [lax.rem(lax.div(self.dp, 2**bit), 2) for bit in range(4)]
        self.core = (self.dp, 1 - self.me)

    def across(self, bit):
        return (self.dp + 2**bit * (1 - 2 * self.bits[bit]), self.me)

    def side(self, step, kind):
        x, y = self.bits[:2]
        return x + kind * (y - x) if step == 0 else y + kind * (x - y)

    def partner(self, step, kind):
        apart = 1 + kind if step == 0 else 2 - kind
        return (self.dp + apart * (1 - 2 * self.side(step, kind)), self.me)

    def along_z(self, mask):
        _, _, low, high = self.bits
        low = 1 - low if mask & 1 else low
        high = 1 - high if mask & 2 else high
        z = 2 * high + low
        return z, (z * 4 + lax.rem(self.dp, 4), self.me)


class GradientSum:
    def __init__(self, ring, keep, outs, ins, done, sems):
        self.ring, self.keep, self.outs, self.ins, self.done = ring, keep, outs, ins, done
        self.sends, self.recvs = sems[:6], sems[6:]
        self.size = done.shape[1]

    def kept_quarter(self, kind, mine):
        side = self.ring.side(1, kind)
        return (side if mine else 1 - side) * (self.size // 4)

    def kept_piece(self, kind, z):
        return pl.ds(aligned(self.kept_quarter(kind, True) + z * (self.size // 16), 16), self.size // 16)

    def finished(self, step, kind):
        at = self.ring.side(0, kind) * (self.size // 2)
        if step > 0:
            at = at + self.ring.side(1, kind) * (self.size // 4)
        if step > 1:
            at = at + self.ring.along_z(0)[0] * (self.size // 16)
        return pl.ds(aligned(at, 16), self.size // (2, 4, 16)[step])

    def down(self, step, j, kind):
        if step < 2:
            return [
                remote(
                    self.outs[step].at[j],
                    self.ins[step].at[j],
                    self.sends[step].at[j],
                    self.recvs[step].at[j],
                    self.ring.partner(step, kind),
                )
            ]
        return [
            remote(
                self.outs[2].at[j, mask - 1],
                self.ins[2].at[j, mask - 1],
                self.sends[2].at[j, mask - 1],
                self.recvs[2].at[j, mask - 1],
                self.ring.along_z(mask)[1],
            )
            for mask in (1, 2, 3)
        ]

    def back(self, step, j, kind):
        rows = self.done.at[j, self.finished(step, kind)]
        sends, recvs = self.sends[5 - step], self.recvs[5 - step]
        if step < 2:
            return [remote(rows, rows, sends.at[j], recvs.at[j], self.ring.partner(step, kind))]
        return [
            remote(rows, rows, sends.at[j, mask - 1], recvs.at[j, mask - 1], self.ring.along_z(mask)[1])
            for mask in (1, 2, 3)
        ]

    def stage(self, number, j, kind):
        quarter = self.size // 4
        if number:
            for copy in self.down(number - 1, j, kind) if number < 4 else self.back(6 - number, j, kind):
                copy.wait()
        if number == 1:
            mine = pl.ds(aligned(self.kept_quarter(kind, True), 16), quarter)
            sent = pl.ds(aligned(self.kept_quarter(kind, False), 16), quarter)
            self.keep[j, mine, :] = self.keep[j, mine, :] + self.ins[0][j, mine, :].astype(F32)
            self.outs[1][j] = (self.keep[j, sent, :] + self.ins[0][j, sent, :].astype(F32)).astype(BF16)
        elif number == 2:
            mine = pl.ds(aligned(self.kept_quarter(kind, True), 16), quarter)
            self.keep[j, mine, :] = self.keep[j, mine, :] + self.ins[1][j].astype(F32)
            for mask in (1, 2, 3):
                self.outs[2][j, mask - 1] = self.keep[j, self.kept_piece(kind, self.ring.along_z(mask)[0]), :].astype(BF16)
        elif number == 3:
            total = self.keep[j, self.kept_piece(kind, self.ring.along_z(0)[0]), :]
            for mask in (1, 2, 3):
                total = total + self.ins[2][j, mask - 1].astype(F32)
            self.done[j, self.finished(2, kind), :] = total.astype(BF16)
        if number < 6:
            for copy in self.down(number, j, kind) if number < 3 else self.back(5 - number, j, kind):
                copy.start()

    def run(self, number, first, count):
        def body(index):
            j = first + index
            self.stage(number, j, lax.rem(j, 2))

        loop(count, body)


def net_kernel(
    sizes,
    videos,
    frames_hbm,
    cot_hbm,
    weight3_hbm,
    weight4_hbm,
    bias3,
    bias4,
    counts,
    conv_hbm,
    frames_grad_hbm,
    grad4_hbm,
    grad3_hbm,
    bias_grads,
    frames,
    cot,
    kept3,
    kept4,
    flat,
    slabs,
    field,
    mid,
    shifted4,
    outgoing,
    incoming,
    last_in,
    frames_field,
    left,
    right,
    alive,
    stash,
    result,
    bias_sum,
    bias_in,
    keep,
    done,
    out0,
    out1,
    out2,
    in0,
    in1,
    in2,
    load_sems,
    kept3_sems,
    kept4_sems,
    frame_sems,
    mid_send,
    mid_recv,
    out_send,
    out_recv,
    last_send,
    last_recv,
    bias_send,
    bias_recv,
    store_sems,
    block_sems,
    *sum_sems,
):
    ring = Ring()
    me = ring.me
    pitch, wide, narrow = sizes.pitch, sizes.own_mid, sizes.own_in
    slab = sizes.slab
    shifted3 = mid

    own_load = pltpu.make_async_copy(frames_hbm, frames.at[0], load_sems.at[0])
    cot_load = pltpu.make_async_copy(cot_hbm, cot, load_sems.at[1])
    kept3_loads = weight_copies(me, weight3_hbm, kept3, kept3_sems, narrow)
    kept4_loads = weight_copies(me, weight4_hbm, kept4, kept4_sems, wide)
    own_load.start()
    barrier = pltpu.get_barrier_semaphore()
    partners = [ring.core, ring.across(0), ring.across(1)] + [ring.along_z(mask)[1] for mask in (1, 2, 3)]
    for partner in partners:
        pl.semaphore_signal(barrier, inc=1, device_id=partner, device_id_type=MESH)
    for copy in [cot_load] + kept3_loads + kept4_loads:
        copy.start()
    for y in range(MAP):
        slabs[(y + 1) * pitch - 16 : (y + 1) * pitch, :] = jnp.zeros((16, wide), F32)

    def bring(source, lanes, target):
        def widen(rows):
            flat[rows, lanes] = source[rows, :].astype(F32)

        windows(sizes, widen)
        to_slabs(sizes, flat, slabs, lanes)

        def pack(y):
            rows = pl.ds(aligned(y * pitch, 16), pitch)
            target[rows, lanes] = slabs[rows, lanes].astype(BF16)

        loop(MAP, pack)

    own_load.wait()
    bring(frames.at[0], slice(0, narrow), field)
    pl.semaphore_wait(barrier, len(partners))
    swap_frames = remote(frames_hbm, frames.at[1], frame_sems.at[0], frame_sems.at[1], ring.core)
    swap_frames.start()
    frame, used, has_left, has_right = column_masks(sizes, wide)
    per_video = sizes.frames // videos
    live = None
    for v in range(videos):
        low = v * per_video - 0.5
        here = (frame > low) & (frame < low + per_video) & (frame < low + counts[v].astype(F32))
        live = here if live is None else live | here
    left[...] = has_left.astype(F32)
    right[...] = has_right.astype(F32)
    alive[...] = (live & used).astype(F32)
    bias_sum[...] = jnp.zeros(bias_sum.shape, F32)
    cot_load.wait()
    bring(cot, slice(0, wide), outgoing)
    swap_frames.wait()
    bring(frames.at[1], slice(narrow, 2 * narrow), field)
    for copy in kept3_loads:
        copy.wait()

    def swap_mid(number):
        rows = sizes.slabs(*THIRDS[number])
        return remote(
            mid.at[rows, 0:wide], mid.at[rows, wide : 2 * wide], mid_send.at[number], mid_recv.at[number], ring.core
        )

    def joined(terms, bias):
        minus, centre, plus = terms
        return centre + before(minus) * left[...] + after(plus) * right[...] + bias[...].astype(F32).reshape(1, -1)

    def finish3(y, terms):
        value = joined(terms, bias3)
        sigma = sigmoid(value)
        mid[slab(y), 0:wide] = (value * sigma).astype(BF16)
        flat[slab(y), :] = silu_slope(value, sigma)
        for number, (_, end) in enumerate(THIRDS):
            if y == end - 1:
                swap_mid(number).start()

    waiting = None
    for y in range(MAP):
        terms = conv_terms(sizes, field, kept3, y, sizes.c_in)
        if waiting is not None:
            finish3(*waiting)
        waiting = (y, terms)
    finish3(*waiting)

    def shift_out(target, y, rounded):
        grad = rounded.astype(F32)
        target[slab(y), 0:wide] = (after(grad) * right[...]).astype(BF16)
        target[slab(y), wide : 2 * wide] = rounded
        target[slab(y), 2 * wide : 3 * wide] = (before(grad) * left[...]).astype(BF16)
        return fold(grad)

    def finish4(y, terms):
        value = joined(terms, bias4)
        sigma = sigmoid(value)
        on = alive[...]
        slabs[slab(y), :] = on * value * sigma
        return shift_out(
            shifted4, y, (outgoing[slab(y), :].astype(F32) * on * silu_slope(value, sigma)).astype(BF16)
        )

    for copy in kept4_loads:
        copy.wait()
    summed = jnp.zeros((8, wide), F32)
    waiting = None
    for y in range(MAP):
        if y == 0:
            swap_mid(0).wait()
            swap_mid(1).wait()
        if y == THIRDS[1][1] - 1:
            swap_mid(2).wait()
            swap_mid(3).wait()
        terms = conv_terms(sizes, mid, kept4, y, sizes.c_mid)
        if waiting is not None:
            summed = summed + finish4(*waiting)
        waiting = (y, terms)
    bias_sum[:, 0:wide] = summed + finish4(*waiting)

    total = GradientSum(ring, keep, (out0, out1, out2), (in0, in1, in2), done, sum_sems)
    run = total.run
    half = sizes.tall // 2

    def give(value, number):
        result[...] = value
        for part in range(2):
            side = ring.side(0, (number + part) % 2)
            lanes = slice(part * LANES, (part + 1) * LANES)
            keep[number + part] = result[pl.ds(aligned(side * half, 16), half), lanes]
            out0[number + part] = result[pl.ds(aligned((1 - side) * half, 16), half), lanes].astype(BF16)
            total.stage(0, number + part, (number + part) % 2)

    step = 0
    events = EVENTS["kernel4"]
    for r in range(3):
        for part in range(sizes.c_mid // WINDOW):
            lanes = slice(part * WINDOW, (part + 1) * WINDOW)
            give(kernel_gradient(sizes, shifted4, mid, r, lanes), 2 * step)
            for event in events.get(step, ()):
                run(*event)
            step += 1

    def swap4(number):
        rows = sizes.slabs(*PAIRS[number])
        return remote(outgoing.at[rows], incoming.at[rows], out_send.at[number], out_recv.at[number], ring.core)

    def finish_back(y):
        value = stash[y % 6] + incoming[slab(y), :].astype(F32)
        return shift_out(shifted3, y, (value * flat[slab(y), :]).astype(BF16))

    summed = jnp.zeros((8, wide), F32)
    events = EVENTS["input4"]
    for number in range(len(PAIRS) + 2):
        if number >= 2:
            swap4(number - 2).wait()
        late = list(range(*PAIRS[number - 2])) if number >= 2 else []
        for y in range(*PAIRS[number]) if number < len(PAIRS) else ():
            grad = input_gradient(sizes, shifted4, kept4, y)
            stash[y % 6] = grad[:, 0:wide]
            outgoing[slab(y), :] = grad[:, wide : 2 * wide].astype(BF16)
            if late:
                summed = summed + finish_back(late.pop(0))
        for y in late:
            summed = summed + finish_back(y)
        if number < len(PAIRS):
            swap4(number).start()
        for event in events.get(number, ()):
            run(*event)
    bias_sum[:, wide : 2 * wide] = summed

    def swap_bias(bit):
        return remote(bias_sum, bias_in.at[bit], bias_send.at[bit], bias_recv.at[bit], ring.across(bit))

    def add_bias(bit):
        swap_bias(bit).wait()
        bias_sum[...] = bias_sum[...] + bias_in[bit]

    swap_bias(0).start()
    events = EVENTS["kernel3"]
    for r in range(3):
        give(kernel_gradient(sizes, shifted3, field, r, slice(0, sizes.c_in)), 2 * step)
        for event in events.get(r, ()):
            run(*event)
        step += 1

    from_slabs(sizes, slabs, flat, slice(0, wide))

    def narrow_down(rows):
        cot[rows, :] = flat[rows, :].astype(BF16)

    windows(sizes, narrow_down)
    conv_store = pltpu.make_async_copy(cot, conv_hbm, store_sems.at[0])
    conv_store.start()
    add_bias(0)
    swap_bias(1).start()
    for event in EVENTS["between"]:
        run(*event)

    def swap3(number):
        rows = sizes.slabs(*THIRDS[number])
        return remote(
            outgoing.at[rows, 0:narrow], last_in.at[rows], last_send.at[number], last_recv.at[number], ring.core
        )

    events = EVENTS["input3"]
    for y in range(MAP):
        grad = input_gradient(sizes, shifted3, kept3, y)
        slabs[slab(y), 0:narrow] = grad[:, 0:narrow]
        outgoing[slab(y), 0:narrow] = grad[:, narrow : 2 * narrow].astype(BF16)
        for number, (_, end) in enumerate(THIRDS):
            if y == end - 1:
                swap3(number).start()
        for event in events.get(y, ()):
            run(*event)
    add_bias(1)
    swap_bias(2).start()
    for number in range(len(THIRDS)):
        swap3(number).wait()

    def join(y):
        rows = pl.ds(aligned(y * pitch, 16), pitch)
        slabs[rows, 0:narrow] = slabs[rows, 0:narrow] + last_in[rows, :].astype(F32)

    loop(MAP, join)
    from_slabs(sizes, slabs, frames_field, slice(0, narrow))
    frames_store = pltpu.make_async_copy(frames_field, frames_grad_hbm, store_sems.at[1])
    frames_store.start()

    def block_stores(j, grad_hbm, first, parts):
        r, part = lax.div(j - first, parts), lax.rem(j - first, parts)
        column_block = lax.rem(part + me * (parts // 2), parts)
        out = []
        for s in range(3):
            at = aligned(((r * 3 + s) * parts + column_block) * LANES, LANES)
            out.append(
                pltpu.make_async_copy(
                    done.at[j, pl.ds(s * wide, wide)], grad_hbm.at[:, pl.ds(at, LANES)], block_sems.at[j, s]
                )
            )
        return out

    def stores4(j):
        return block_stores(j, grad4_hbm, 0, sizes.c_mid // LANES)

    def stores3(j):
        return block_stores(j, grad3_hbm, sizes.blocks4, sizes.c_in // LANES)

    def save(stores, first, count):
        def body(index):
            j = first + index
            total.stage(6, j, lax.rem(j, 2))
            for copy in stores(j):
                copy.start()

        loop(count, body)

    def saved(stores, first, count):
        def body(index):
            for copy in stores(first + index):
                copy.wait()

        loop(count, body)

    for place, event in enumerate(EVENTS["last"]):
        if place == 8:
            add_bias(2)
            swap_bias(3).start()
        if place == 16:
            add_bias(3)
        if event[0] == 6:
            save(stores4 if event[1] < sizes.blocks4 else stores3, event[1], event[2])
        else:
            run(*event)
    bias_grads[...] = jnp.sum(bias_sum[...], axis=0, keepdims=True)
    conv_store.wait()
    frames_store.wait()
    saved(stores4, 0, sizes.blocks4)
    saved(stores3, sizes.blocks4, sizes.blocks3)


THIRDS = ((0, 4), (4, 7), (7, 10), (10, 13))
PAIRS = tuple((y, min(y + 2, MAP)) for y in range(0, MAP, 2))
EVENTS = {
    "kernel4": {
        3: [(1, 0, 2)],
        4: [(1, 2, 2)],
        5: [(1, 4, 2)],
    },
    "input4": {
        0: [(1, 6, 2)],
        1: [(2, 0, 2)],
        2: [(1, 8, 2), (2, 2, 2)],
        3: [(1, 10, 2), (2, 4, 2)],
        4: [(3, 0, 2), (2, 6, 2), (2, 8, 2)],
        5: [(3, 2, 2), (2, 10, 2)],
        6: [(3, 4, 2)],
        8: [(4, 0, 2)],
    },
    "kernel3": {
        0: [(3, 6, 2)],
        1: [(3, 8, 2), (5, 0, 2)],
        2: [(4, 2, 2), (1, 12, 2), (3, 10, 2)],
    },
    "between": [(4, 4, 2), (1, 14, 2)],
    "input3": {
        3: [(4, 6, 2)],
        7: [(4, 8, 2), (1, 16, 2)],
        9: [(5, 2, 2)],
        11: [(4, 10, 2), (2, 12, 2)],
    },
    "last": [
        (6, 0, 2), (5, 4, 2), (2, 14, 2), (5, 6, 2), (5, 8, 2), (2, 16, 2), (3, 12, 2), (6, 2, 2),
        (5, 10, 2), (3, 14, 2), (6, 4, 2), (3, 16, 2), (6, 6, 2), (4, 12, 2), (6, 8, 2), (4, 14, 2),
        (6, 10, 2), (4, 16, 2), (5, 12, 2), (5, 14, 2), (5, 16, 2), (6, 12, 2), (6, 14, 2), (6, 16, 2),
    ],
}


def net(sizes, videos, frames, cot, weight3, weight4, bias3, bias4, counts):
    any_spec = pl.BlockSpec(memory_space=pl.ANY)
    vmem = pl.BlockSpec(memory_space=pltpu.VMEM)
    smem = pl.BlockSpec(memory_space=pltpu.SMEM)
    wide, narrow, pitch, rows, tall = sizes.own_mid, sizes.own_in, sizes.pitch, sizes.rows, sizes.tall
    blocks = sizes.blocks
    dma = pltpu.SemaphoreType.DMA
    return pl.pallas_call(
        functools.partial(net_kernel, sizes, videos),
        out_shape=(
            jax.ShapeDtypeStruct((sizes.columns, wide), BF16),
            jax.ShapeDtypeStruct((sizes.columns, narrow), F32),
            jax.ShapeDtypeStruct((wide, 9 * sizes.c_mid), BF16),
            jax.ShapeDtypeStruct((wide, 9 * sizes.c_in), BF16),
            jax.ShapeDtypeStruct((1, 2 * wide), F32),
        ),
        in_specs=[any_spec] * 4 + [vmem, vmem, smem],
        out_specs=(any_spec,) * 4 + (vmem,),
        scratch_shapes=[
            pltpu.VMEM((2, sizes.columns, narrow), BF16),
            pltpu.VMEM((sizes.columns, wide), BF16),
            pltpu.VMEM((3, tall, sizes.c_in), BF16),
            pltpu.VMEM((3, tall, sizes.c_mid), BF16),
            pltpu.VMEM((rows, wide), F32),
            pltpu.VMEM((rows, wide), F32),
            pltpu.VMEM((rows, sizes.c_in), BF16),
            pltpu.VMEM((rows, tall), BF16),
            pltpu.VMEM((rows, tall), BF16),
            pltpu.VMEM((rows, wide), BF16),
            pltpu.VMEM((rows, wide), BF16),
            pltpu.VMEM((rows, narrow), BF16),
            pltpu.VMEM((sizes.columns, narrow), F32),
            pltpu.VMEM((pitch, wide), F32),
            pltpu.VMEM((pitch, wide), F32),
            pltpu.VMEM((pitch, wide), F32),
            pltpu.VMEM((6, pitch, wide), F32),
            pltpu.VMEM((tall, WINDOW), F32),
            pltpu.VMEM((8, 2 * wide), F32),
            pltpu.VMEM((4, 8, 2 * wide), F32),
            pltpu.VMEM((blocks, tall // 2, LANES), F32),
            pltpu.VMEM((blocks, tall, LANES), BF16),
        ]
        + [
            pltpu.VMEM((blocks, tall // 2, LANES), BF16),
            pltpu.VMEM((blocks, tall // 4, LANES), BF16),
            pltpu.VMEM((blocks, 3, tall // 16, LANES), BF16),
        ]
        * 2
        + [
            dma((2,)),
            dma((18,)),
            dma((18,)),
            dma((2,)),
            dma((MAP,)),
            dma((MAP,)),
            dma((MAP,)),
            dma((MAP,)),
            dma((MAP,)),
            dma((MAP,)),
            dma((4,)),
            dma((4,)),
            dma((2,)),
            dma((blocks, 3)),
        ]
        + [dma((blocks,)), dma((blocks,)), dma((blocks, 3)), dma((blocks, 3)), dma((blocks,)), dma((blocks,))] * 2,
        compiler_params=pltpu.CompilerParams(collective_id=0, has_side_effects=True, vmem_limit_bytes=63 * MIB),
        cost_estimate=pl.CostEstimate(flops=45 * 10**9, bytes_accessed=3 * 10**7, transcendentals=2 * 10**6),
    )(frames, cot, weight3, weight4, bias3, bias4, counts)


def end_kernel(conv, frames_grad, grad3, grad4, biases, conv_out, frames_out, wide3, bias3, wide4, bias4, *scratch):
    narrow3, narrow4, full3, full4, conv_kept, frames_kept, load_sems, store_sems = scratch
    passed = []
    for number, (source, kept, target) in enumerate(((conv, conv_kept, conv_out), (frames_grad, frames_kept, frames_out))):
        passed.append(
            (
                pltpu.make_async_copy(source, kept, load_sems.at[number]),
                pltpu.make_async_copy(kept, target, store_sems.at[number]),
            )
        )
    parts = []
    for source, small, large, target in ((grad4, narrow4, full4, wide4), (grad3, narrow3, full3, wide3)):
        span = source.shape[1] // 3
        for part in range(3):
            lanes = pl.ds(part * span, span)
            at = 2 + len(parts)
            parts.append(
                (
                    pltpu.make_async_copy(source.at[:, lanes], small.at[:, lanes], load_sems.at[at]),
                    small,
                    large,
                    lanes,
                    pltpu.make_async_copy(large.at[:, lanes], target.at[:, lanes], store_sems.at[at]),
                )
            )
    for part in parts:
        part[0].start()
    for load, _ in passed:
        load.start()
    half = biases.shape[1] // 2
    bias4[...] = biases[0, 0:half]
    bias3[...] = biases[0, half:]
    for load, small, large, lanes, store in parts:
        load.wait()
        large[:, lanes] = small[:, lanes].astype(F32)
        store.start()
    for load, store in passed:
        load.wait()
        store.start()
    for part in parts:
        part[4].wait()
    for _, store in passed:
        store.wait()


def end(conv, frames_grad, grad3, grad4, biases):
    any_spec = pl.BlockSpec(memory_space=pl.ANY)
    vmem = pl.BlockSpec(memory_space=pltpu.VMEM)
    bias = jax.ShapeDtypeStruct((biases.shape[1] // 2,), F32)
    dma = pltpu.SemaphoreType.DMA
    return pl.pallas_call(
        end_kernel,
        out_shape=(
            jax.ShapeDtypeStruct(conv.shape, conv.dtype),
            jax.ShapeDtypeStruct(frames_grad.shape, F32),
            jax.ShapeDtypeStruct(grad3.shape, F32),
            bias,
            jax.ShapeDtypeStruct(grad4.shape, F32),
            bias,
        ),
        in_specs=[any_spec] * 4 + [vmem],
        out_specs=(any_spec, any_spec, any_spec, vmem, any_spec, vmem),
        scratch_shapes=[
            pltpu.VMEM(grad3.shape, BF16),
            pltpu.VMEM(grad4.shape, BF16),
            pltpu.VMEM(grad3.shape, F32),
            pltpu.VMEM(grad4.shape, F32),
            pltpu.VMEM(conv.shape, conv.dtype),
            pltpu.VMEM(frames_grad.shape, F32),
            dma((8,)),
            dma((8,)),
        ],
        compiler_params=pltpu.CompilerParams(vmem_limit_bytes=63 * MIB),
        cost_estimate=pl.CostEstimate(flops=10**7, bytes_accessed=2 * 10**7, transcendentals=0),
    )(conv, frames_grad, grad3, grad4, biases)


def kernel_device(frames, clip_counts, conv3_weight, conv3_bias, conv4_weight, conv4_bias, cotangent):
    sizes = Sizes(frames.shape[1], 2, conv3_weight.shape[1] // 9, conv4_weight.shape[1] // 9)
    results = net(
        sizes,
        clip_counts.shape[0],
        frames.T,
        cotangent.T,
        conv3_weight,
        conv4_weight,
        conv3_bias,
        conv4_bias,
        clip_counts,
    )
    conv4_out, frames_grad, grad3, bias3, grad4, bias4 = end(
        results[0], results[1], results[3], results[2], results[4]
    )
    return conv4_out.T, frames_grad.T, grad3, bias3, grad4, bias4


def solution(mesh):
    in_specs = (
        P("chan", "dp"),
        P("dp"),
        P("chan", None),
        P("chan"),
        P("chan", None),
        P("chan"),
        P("chan", "dp"),
    )
    out_specs = (
        P("chan", "dp"),
        P("chan", "dp"),
        P("chan", None),
        P("chan"),
        P("chan", None),
        P("chan"),
    )
    fits = mesh.shape["chan"] == 2 and mesh.shape["dp"] == 16
    per_device = kernel_device if fits else general_device
    return jax.shard_map(
        per_device, mesh=mesh, in_specs=in_specs, out_specs=out_specs, check_vma=False
    )
```
